32 devices in a mesh: tx: 4 (over z), ty: 8 (over y, x, core).
Axes of the slice: x: 2, y: 2, z: 4, core: 2. Of those that a mesh axis runs over, the one named last changes fastest.
Arguments:
- hidden_in: bfloat16 [128, 8192], P(None, ('ty', 'tx'))
- norm_gain: bfloat16 [8192], P(('ty', 'tx')), may hold values from 0.5 to 1.5
- qkv_weight: bfloat16 [8192, 10240], P('ty', 'tx'), may hold values from -0.0625 to 0.0625
- qkv_bias: bfloat16 [10240], replicated, may hold values from -4 to 4
- key_cache: bfloat16 [128, 128, 1024], P(('ty', 'tx')), may hold values from -6 to 6
- value_cache: bfloat16 [128, 128, 1024], P(('ty', 'tx')), may hold values from -6 to 6
- lengths: int32 [128], P(('ty', 'tx')), may hold values from 1 to 128
- out_weight: bfloat16 [8192, 8192], P('tx', 'ty'), may hold values from -0.0625 to 0.0625
- final_gain: bfloat16 [8192], P(('ty', 'tx')), may hold values from 0.5 to 1.5
- in_weight: bfloat16 [8192, 2048], P('ty', 'tx'), may hold values from -0.0625 to 0.0625
- owners: int32 [128], replicated, may hold values from 0 to 7, as said below
- codebook_ids: int32 [128, 8], replicated, may hold values from 0 to 1023
- mlp_gate: bfloat16 [2048, 4096], P(None, 'tx'), may hold values from -0.125 to 0.125
- mlp_up: bfloat16 [2048, 4096], P(None, 'tx'), may hold values from -0.125 to 0.125
- mlp_down: bfloat16 [4096, 2048], P('tx'), may hold values from -0.09375 to 0.09375
- pre_gain: bfloat16 [2048], replicated, may hold values from 0.5 to 1.5
- head_gain: bfloat16 [2048], replicated, may hold values from 0.5 to 1.5
- codebook_table: bfloat16 [8, 1024, 2048], P(None, 'tx'), may hold values from -0.375 to 0.375
Outputs:
- hidden_out: bfloat16 [128, 8192], P(None, ('ty', 'tx'))
- depth_logprob: float32 [8, 8, 32], P('ty')
The draws below stay inside these ranges and needn't reach their ends.
Inputs may be any that keep to these rules, and one draw needn't show every extreme that they name: `owners`: in each of the 8 aligned blocks of 16 rows no owner is named more than 4 times, and one owner is named exactly 4 times in every block.
All inputs are finite; a program needn't handle non-finite values.
Results may differ from the reference program's by a relative error of at most 0.0095.
Values may be sent and summed in bfloat16 or wider, within the bound.
A program may use at most 128 MiB of HBM per device.

```python
from functools import partial
import jax
import jax.numpy as jnp
from jax import lax

D = 8192
HEADS = 64
KV_HEADS = 8
HEAD_DIM = 128
DW = 2048
DFF = 4096
CB = 1024
STEPS = 8
LMAX = 128
QW = 8192
KW = 1024
QKVW = 10240
ROWS = 128
ROWS_TY = 16
OWNERS = 8
CAP = 4


def draw_hidden_in(key, part):
    key = jax.random.fold_in(key, 11)
    key_base, key_rows = jax.random.split(key, 2)
    row_scale = jnp.exp(jax.random.uniform(key_rows, (ROWS, 1), jnp.float32, jnp.log(0.3), jnp.log(3.0)))
    block_width = D // OWNERS
    column_pos = (jnp.arange(D, dtype=jnp.int32) % block_width).astype(jnp.float32) / (block_width - 1)
    base_values = jax.random.normal(key_base, (ROWS, D), jnp.float32)
    column_scale = 0.15 * jnp.exp(jnp.log(10.0) * column_pos)
    return (base_values * row_scale * column_scale[None, :]).astype(jnp.bfloat16)


def owner_block(hot_owner, block_key):
    key_order, key_pool = jax.random.split(block_key)
    other_pool = (hot_owner + 1 + jnp.arange((OWNERS - 1) * CAP, dtype=jnp.int32) // CAP) % OWNERS
    other_pool = jax.random.permutation(key_pool, other_pool)
    assigned = jnp.concatenate([jnp.full((CAP,), hot_owner, jnp.int32), other_pool[:ROWS_TY - CAP]])
    placing = jax.random.permutation(key_order, ROWS_TY)
    return assigned[jnp.argsort(placing)].astype(jnp.int32)


def draw_owners(key, part):
    key = jax.random.fold_in(key, 23)
    key_hot, key_blocks = jax.random.split(key)
    hot_owner = jax.random.randint(key_hot, (), 0, OWNERS, jnp.int32)
    block_keys = jax.random.split(key_blocks, OWNERS)
    return jax.vmap(partial(owner_block, hot_owner))(block_keys).reshape(ROWS)


def plant(drawn, rng, low, top_value):
    longest = drawn.shape.index(max(drawn.shape))
    spots = []
    for shift in (0, 1):
        where = [jax.random.randint(jax.random.fold_in(rng, axis), (), 0, length) for axis, length in enumerate(drawn.shape)]
        where[longest] = (where[longest] + shift) % drawn.shape[longest]
        spots.append(tuple(where))
    return drawn.at[spots[0]].set(low).at[spots[1]].set(top_value)


def level_of(rng, dims, pieces, least, largest):
    factor_of, own = 1.0, jax.random.fold_in(rng, 6)
    for axis_at, shards_of in pieces:
        draws = jnp.exp(jax.random.uniform(jax.random.fold_in(own, axis_at), (shards_of,), jnp.float32, least / len(pieces), largest / len(pieces)))
        factor_of = factor_of * jnp.repeat(draws, dims[axis_at] // shards_of).reshape([-1 if axis == axis_at else 1 for axis in range(len(dims))])
    return factor_of


def bell_draw(rng, extent, width, reach, shards=(), kind=jnp.bfloat16):
    array = width * jax.random.normal(rng, extent, jnp.float32)
    if shards:
        array = array * level_of(rng, extent, shards, -0.22, 0.18)
    return jnp.clip(array, -reach, reach).astype(kind)


def setup_inputs(seed: int = 0) -> dict:
    key_of = jax.random.split(jax.random.key(seed), 19)
    return {
        "hidden_in": draw_hidden_in(jax.random.fold_in(key_of[18], 71), 0),
        "norm_gain": jnp.clip(1.0 + 0.1 * jax.random.normal(key_of[1], (D,), jnp.float32), 0.5, 1.5).astype(jnp.bfloat16),
        "qkv_weight": bell_draw(key_of[2], (D, QKVW), D ** -0.5, 0.0625, ((0, 8), (1, 4))),
        "qkv_bias": bell_draw(key_of[3], (QKVW,), 1.0, 4.0),
        "key_cache": bell_draw(key_of[4], (ROWS, LMAX, KW), 1.0, 6.0, ((0, 32),)),
        "value_cache": bell_draw(key_of[5], (ROWS, LMAX, KW), 1.0, 6.0, ((0, 32),)),
        "lengths": plant(jax.random.randint(key_of[6], (ROWS,), 1, LMAX + 1), jax.random.fold_in(key_of[6], 1), 1, LMAX).astype(jnp.int32),
        "out_weight": bell_draw(key_of[7], (QW, D), QW ** -0.5, 0.0625, ((0, 4), (1, 8))),
        "final_gain": jnp.clip(1.0 + 0.1 * jax.random.normal(key_of[8], (D,), jnp.float32), 0.5, 1.5).astype(jnp.bfloat16),
        "in_weight": bell_draw(key_of[9], (D, DW), D ** -0.5, 0.0625, ((0, 8), (1, 4))),
        "owners": draw_owners(jax.random.fold_in(key_of[18], 71), 0),
        "codebook_ids": plant(jax.random.randint(key_of[11], (ROWS, STEPS), 0, CB), jax.random.fold_in(key_of[11], 1), 0, CB - 1).astype(jnp.int32),
        "mlp_gate": bell_draw(key_of[12], (DW, DFF), DW ** -0.5, 0.125, ((1, 4),)),
        "mlp_up": bell_draw(key_of[13], (DW, DFF), DW ** -0.5, 0.125, ((1, 4),)),
        "mlp_down": bell_draw(key_of[14], (DFF, DW), DFF ** -0.5, 0.09375, ((0, 4),)),
        "pre_gain": jnp.clip(1.0 + 0.1 * jax.random.normal(key_of[15], (DW,), jnp.float32), 0.5, 1.5).astype(jnp.bfloat16),
        "head_gain": jnp.clip(1.0 + 0.1 * jax.random.normal(key_of[16], (DW,), jnp.float32), 0.5, 1.5).astype(jnp.bfloat16),
        "codebook_table": bell_draw(key_of[17], (STEPS, CB, DW), (DW // 9) ** -0.5, 0.375, ((1, 4),)),
    }


epsilon = 1e-06
rope_base = 1000000.0
embed_gain = 16.0

def rms_scale(values, gain):
    mean_square = lax.optimization_barrier(jnp.mean(values * values, axis=-1, keepdims=True))
    return values * lax.rsqrt(mean_square + epsilon) * gain.astype(jnp.float32)

def rotate(values, position):
    half_dim = values.shape[-1] // 2
    frequency = jnp.exp(-jnp.log(rope_base) * (2.0 * jnp.arange(half_dim, dtype=jnp.float32) / values.shape[-1]))
    phase_angle = position.astype(jnp.float32)[:, None, None] * frequency[None, None, :]
    cosine = jnp.cos(phase_angle)
    sine_part = jnp.sin(phase_angle)
    first_half = values[..., :half_dim]
    second_half = values[..., half_dim:]
    return jnp.concatenate([first_half * cosine - second_half * sine_part, second_half * cosine + first_half * sine_part], axis=-1)

def attend(query_heads, new_key, new_value, key_cache, value_cache, lengths):
    row_count = query_heads.shape[0]
    group_size = HEADS // KV_HEADS
    query_heads = query_heads.reshape(row_count, KV_HEADS, group_size, HEAD_DIM).astype(jnp.float32)
    keys_all = key_cache.reshape(row_count, LMAX, KV_HEADS, HEAD_DIM).astype(jnp.float32)
    values_all = value_cache.reshape(row_count, LMAX, KV_HEADS, HEAD_DIM).astype(jnp.float32)
    scores = jnp.einsum('rgjd,rtgd->rgjt', query_heads, keys_all)
    own_score = jnp.einsum('rgjd,rgd->rgj', query_heads, new_key.astype(jnp.float32))
    in_cache = jnp.arange(LMAX, dtype=jnp.int32)[None, :] < lengths[:, None]
    weights = jnp.where(in_cache[:, None, None, :], jnp.exp(scores), 0.0)
    own_weight = jnp.exp(own_score)
    denominator = lax.optimization_barrier(jnp.sum(weights, axis=-1)) + own_weight
    probability = (weights / denominator[..., None]).astype(jnp.bfloat16)
    own_prob = (own_weight / denominator).astype(jnp.bfloat16)
    blended = jnp.einsum('rgjt,rtgd->rgjd', probability.astype(jnp.float32), values_all)
    blended = blended + own_prob.astype(jnp.float32)[..., None] * new_value.astype(jnp.float32)[:, :, None, :]
    return blended.reshape(row_count, HEADS * HEAD_DIM).astype(jnp.bfloat16)

def depth_rows(start_rows, codebook_ids, mlp_gate, mlp_up, mlp_down, pre_gain, head_gain, codebook_table):
    depth_state = start_rows.astype(jnp.float32)
    columns = []
    for step_index in range(STEPS):
        inner_rows = rms_scale(depth_state, pre_gain).astype(jnp.bfloat16)
        gate_part = jnp.dot(inner_rows, mlp_gate, preferred_element_type=jnp.float32)
        up_part = jnp.dot(inner_rows, mlp_up, preferred_element_type=jnp.float32)
        activation = (jax.nn.silu(gate_part) * up_part).astype(jnp.bfloat16)
        depth_state = depth_state + jnp.dot(activation, mlp_down, preferred_element_type=jnp.float32)
        outer_rows = rms_scale(depth_state, head_gain).astype(jnp.bfloat16)
        logits = jnp.dot(outer_rows, codebook_table[step_index].T, preferred_element_type=jnp.float32)
        picked = jnp.take_along_axis(logits, codebook_ids[:, step_index:step_index + 1], axis=1)[:, 0]
        columns.append(picked - jnp.log(lax.optimization_barrier(jnp.sum(jnp.exp(logits), axis=1))))
        if step_index + 1 < STEPS:
            embedded = codebook_table[step_index][codebook_ids[:, step_index]].astype(jnp.float32)
            depth_state = depth_state + embed_gain * embedded
    return jnp.stack(columns, axis=1)

def reference(hidden_in, norm_gain, qkv_weight, qkv_bias, key_cache, value_cache, lengths, out_weight, final_gain, in_weight, owners, codebook_ids, mlp_gate, mlp_up, mlp_down, pre_gain, head_gain, codebook_table):
    residual = hidden_in.astype(jnp.float32)
    normed = rms_scale(residual, norm_gain).astype(jnp.bfloat16)
    qkv_raw = jnp.dot(normed, qkv_weight, preferred_element_type=jnp.float32).astype(jnp.bfloat16)
    qkv = qkv_raw.astype(jnp.float32) + qkv_bias.astype(jnp.float32)
    query_width = HEADS * HEAD_DIM
    key_width = KV_HEADS * HEAD_DIM
    query_heads = rotate(qkv[:, :query_width].reshape(ROWS, HEADS, HEAD_DIM), lengths)
    query_heads = (query_heads * HEAD_DIM ** (-0.5)).astype(jnp.bfloat16)
    new_key = rotate(qkv[:, query_width:query_width + key_width].reshape(ROWS, KV_HEADS, HEAD_DIM), lengths).astype(jnp.bfloat16)
    new_value = qkv[:, query_width + key_width:].reshape(ROWS, KV_HEADS, HEAD_DIM).astype(jnp.bfloat16)
    attended = attend(query_heads, new_key, new_value, key_cache, value_cache, lengths)
    projected = jnp.dot(attended, out_weight, preferred_element_type=jnp.float32)
    hidden_out = (residual + projected).astype(jnp.bfloat16)
    final_rows = rms_scale(hidden_out.astype(jnp.float32), final_gain).astype(jnp.bfloat16)
    depth_start = jnp.dot(final_rows, in_weight, preferred_element_type=jnp.float32).astype(jnp.bfloat16)
    row_logprob = depth_rows(depth_start, codebook_ids, mlp_gate, mlp_up, mlp_down, pre_gain, head_gain, codebook_table)
    member = (owners[:, None] == jnp.arange(OWNERS, dtype=jnp.int32)[None, :]).astype(jnp.int32)
    earlier = jnp.cumsum(member.reshape(OWNERS, ROWS_TY, OWNERS), axis=1).reshape(ROWS, OWNERS) - member
    rank_in_block = lax.optimization_barrier(jnp.sum(earlier * member, axis=1))
    block_index = jnp.arange(ROWS, dtype=jnp.int32) // ROWS_TY
    slot_index = (block_index * CAP + rank_in_block).astype(jnp.int32)
    depth_logprob = jnp.zeros((OWNERS, STEPS, OWNERS * CAP), jnp.float32).at[owners, :, slot_index].set(row_logprob)
    return (hidden_out, depth_logprob)
```

```python
import functools

import jax
import jax.numpy as jnp
from jax import lax
from jax.experimental import pallas as pl
from jax.experimental.pallas import tpu as pltpu
from jax.sharding import PartitionSpec as P

HEADS = 64
KV_HEADS = 8
HEAD_DIM = 128
STEPS = 8
LMAX = 128
LANES = 128
PAD = 16
VMEM_BYTES = 56 * 1024 * 1024
MESH = pl.DeviceIdType.MESH

epsilon = 1e-06
rope_base = 1000000.0
embed_gain = 16.0


def rotate(values, position):
    half_dim = values.shape[-1] // 2
    frequency = jnp.exp(
        -jnp.log(rope_base) * (2.0 * jnp.arange(half_dim, dtype=jnp.float32) / values.shape[-1])
    )
    phase_angle = position.astype(jnp.float32)[:, None, None] * frequency[None, None, :]
    cosine = jnp.cos(phase_angle)
    sine_part = jnp.sin(phase_angle)
    first_half = values[..., :half_dim]
    second_half = values[..., half_dim:]
    return jnp.concatenate(
        [
            first_half * cosine - second_half * sine_part,
            second_half * cosine + first_half * sine_part,
        ],
        axis=-1,
    )


def attend(query_heads, new_key, new_value, key_cache, value_cache, lengths):
    row_count = query_heads.shape[0]
    group_size = HEADS // KV_HEADS
    query_heads = query_heads.reshape(row_count, KV_HEADS, group_size, HEAD_DIM)
    keys_all = key_cache.reshape(row_count, LMAX, KV_HEADS, HEAD_DIM)
    values_all = value_cache.reshape(row_count, LMAX, KV_HEADS, HEAD_DIM)
    scores = jnp.einsum(
        "rgjd,rtgd->rgjt", query_heads, keys_all, preferred_element_type=jnp.float32
    )
    own_score = jnp.einsum(
        "rgjd,rgd->rgj", query_heads, new_key, preferred_element_type=jnp.float32
    )
    in_cache = jnp.arange(LMAX, dtype=jnp.int32)[None, :] < lengths[:, None]
    weights = jnp.where(in_cache[:, None, None, :], jnp.exp(scores), 0.0)
    own_weight = jnp.exp(own_score)
    denominator = jnp.sum(weights, axis=-1) + own_weight
    probability = (weights / denominator[..., None]).astype(jnp.bfloat16)
    own_prob = (own_weight / denominator).astype(jnp.bfloat16)
    blended = jnp.einsum(
        "rgjt,rtgd->rgjd", probability, values_all, preferred_element_type=jnp.float32
    )
    blended = (
        blended
        + own_prob.astype(jnp.float32)[..., None] * new_value.astype(jnp.float32)[:, :, None, :]
    )
    return blended.reshape(row_count, HEADS * HEAD_DIM).astype(jnp.bfloat16)


def split_square(total):
    total = jnp.broadcast_to(total, (total.shape[0], LANES))
    high = total.astype(jnp.bfloat16)
    low = (total - high.astype(jnp.float32)).astype(jnp.bfloat16)
    lane = lax.broadcasted_iota(jnp.int32, total.shape, 1)
    return jnp.where(lane < LANES // 2, high.astype(jnp.float32), low.astype(jnp.float32)).astype(
        jnp.bfloat16
    )


def join_square(block):
    block = block.astype(jnp.float32)
    return block[:, :1] + block[:, LANES // 2 : LANES // 2 + 1]


def push(source, target, send_sem, recv_sem, axis, peer):
    return pltpu.make_async_remote_copy(
        src_ref=source,
        dst_ref=target,
        send_sem=send_sem,
        recv_sem=recv_sem,
        device_id={axis: peer},
        device_id_type=MESH,
    )


def greet(axes):
    barrier = pltpu.get_barrier_semaphore()
    count = 0
    for axis in axes:
        me, size = lax.axis_index(axis), lax.axis_size(axis)
        for step in range(1, size):
            pl.semaphore_signal(
                barrier,
                inc=1,
                device_id={axis: lax.rem(me + step, size)},
                device_id_type=MESH,
            )
        count += size - 1
    pl.semaphore_wait(barrier, count)


def spread_own(buffer, send_sems, recv_sems, axis):
    me, size = lax.axis_index(axis), lax.axis_size(axis)
    for step in range(1, size):
        peer = lax.rem(me + step, size)
        push(
            buffer.at[me], buffer.at[me], send_sems.at[peer], recv_sems.at[me], axis, peer
        ).start()


def deal(source, buffer, send_sems, recv_sems, axis):
    me, size = lax.axis_index(axis), lax.axis_size(axis)
    for step in range(1, size):
        peer = lax.rem(me + step, size)
        push(
            source.at[peer], buffer.at[me], send_sems.at[peer], recv_sems.at[me], axis, peer
        ).start()


def take(buffer, send_sems, recv_sems, axis, step):
    me, size = lax.axis_index(axis), lax.axis_size(axis)
    peer = lax.rem(me + size - step, size)
    push(buffer.at[peer], buffer.at[peer], send_sems.at[peer], recv_sems.at[peer], axis, peer).wait_recv()
    return peer


def take_all(buffer, send_sems, recv_sems, axis):
    for step in range(1, lax.axis_size(axis)):
        take(buffer, send_sems, recv_sems, axis, step)


def settle(buffer, send_sems, recv_sems, axis):
    me, size = lax.axis_index(axis), lax.axis_size(axis)
    for step in range(1, size):
        peer = lax.rem(me + step, size)
        push(buffer.at[peer], buffer.at[peer], send_sems.at[peer], recv_sems.at[me], axis, peer).wait_send()


def gained_rows(blocks, rows, scaled_ref):
    square = jnp.zeros((rows, 1), jnp.float32)
    width = blocks.shape[2]
    for part in range(blocks.shape[0]):
        values = blocks[part, :rows, :].astype(jnp.float32)
        gain = blocks[part, rows : rows + PAD, :].astype(jnp.float32)[:1]
        square = square + jnp.sum(values * values, axis=1, keepdims=True)
        scaled_ref[:, part * width : (part + 1) * width] = (values * gain).astype(jnp.bfloat16)
    return square


def qkv_kernel(
    full_width, entry_ref, weight_hbm, out_ref, weight, gathered, scaled, sums_out, sums_in,
    rows_out, rows_in, weight_sem, g_send, g_recv, s_send, s_recv, r_send, r_recv,
):
    me_tx, me_ty = lax.axis_index("tx"), lax.axis_index("ty")
    count_tx, count_ty = lax.axis_size("tx"), lax.axis_size("ty")
    rows = scaled.shape[0]
    columns = weight.shape[1]
    fetch = pltpu.make_async_copy(weight_hbm, weight, weight_sem)
    fetch.start()
    gathered[me_tx] = entry_ref[...]
    greet(("tx", "ty"))
    spread_own(gathered, g_send, g_recv, "tx")
    take_all(gathered, g_send, g_recv, "tx")
    square = gained_rows(gathered, rows, scaled)
    fetch.wait()
    tile = 512
    block_rows = rows // count_ty
    for start in range(0, columns, tile):
        part = jnp.dot(
            scaled[...], weight[:, start : start + tile], preferred_element_type=jnp.float32
        )
        sums_out[:, :, start : start + tile] = part.astype(jnp.bfloat16).reshape(
            count_ty, block_rows, tile
        )
    sums_out[:, :, columns:] = split_square(square).reshape(count_ty, block_rows, LANES)
    deal(sums_out, sums_in, s_send, s_recv, "ty")
    sums_in[me_ty] = sums_out[me_ty]
    take_all(sums_in, s_send, s_recv, "ty")
    square = jnp.zeros((block_rows, 1), jnp.float32)
    for part in range(count_ty):
        square = square + join_square(sums_in[part, :, columns:])
    scale = lax.rsqrt(square / full_width + epsilon)
    own_rows = block_rows // count_tx
    piece = columns // count_tx
    raw = []
    for q in range(count_tx):
        total = jnp.zeros((block_rows, piece), jnp.float32)
        for part in range(count_ty):
            total = total + sums_in[part, :, q * piece : (q + 1) * piece].astype(jnp.float32)
        raw.append(total * scale)
    for d in range(count_tx):
        rows_out[d] = jnp.concatenate(
            [part[d * own_rows : (d + 1) * own_rows] for part in raw], axis=0
        ).astype(jnp.bfloat16)
    deal(rows_out, rows_in, r_send, r_recv, "tx")
    rows_in[me_tx] = rows_out[me_tx]
    take_all(rows_in, r_send, r_recv, "tx")
    out_ref[...] = rows_in[...]
    settle(gathered, g_send, g_recv, "tx")
    settle(sums_in, s_send, s_recv, "ty")
    settle(rows_in, r_send, r_recv, "tx")


def qkv_rows(entry, qkv_weight, rows, full_width, count_tx, count_ty):
    columns = qkv_weight.shape[1]
    block_rows = rows // count_ty
    piece = columns // count_tx
    dma = pltpu.SemaphoreType.DMA
    return pl.pallas_call(
        functools.partial(qkv_kernel, full_width),
        out_shape=jax.ShapeDtypeStruct((count_tx, block_rows, piece), jnp.bfloat16),
        in_specs=[
            pl.BlockSpec(memory_space=pltpu.VMEM),
            pl.BlockSpec(memory_space=pl.ANY),
        ],
        out_specs=pl.BlockSpec(memory_space=pltpu.VMEM),
        scratch_shapes=[
            pltpu.VMEM(qkv_weight.shape, jnp.bfloat16),
            pltpu.VMEM((count_tx,) + entry.shape, jnp.bfloat16),
            pltpu.VMEM((rows, count_tx * entry.shape[1]), jnp.bfloat16),
            pltpu.VMEM((count_ty, block_rows, columns + LANES), jnp.bfloat16),
            pltpu.VMEM((count_ty, block_rows, columns + LANES), jnp.bfloat16),
            pltpu.VMEM((count_tx, block_rows, piece), jnp.bfloat16),
            pltpu.VMEM((count_tx, block_rows, piece), jnp.bfloat16),
            dma,
            dma((count_tx,)), dma((count_tx,)),
            dma((count_ty,)), dma((count_ty,)),
            dma((count_tx,)), dma((count_tx,)),
        ],
        compiler_params=pltpu.CompilerParams(
            collective_id=1, has_side_effects=True, vmem_limit_bytes=VMEM_BYTES
        ),
    )(entry, qkv_weight)


def out_kernel(
    full_width, att_ref, out_hbm, resid_ref, gain_ref, in_hbm, select_ref, hidden_ref, state_ref,
    out_w, in_w, pieces, blocks, part_out, part_in, gathered, scaled, slots_out, slots_in,
    out_sem, in_sem, a_send, a_recv, b_send, b_recv, p_send, p_recv, g_send, g_recv, s_send, s_recv,
):
    me_tx, me_ty = lax.axis_index("tx"), lax.axis_index("ty")
    count_tx, count_ty = lax.axis_size("tx"), lax.axis_size("ty")
    rows, width = resid_ref.shape
    fetch_out = pltpu.make_async_copy(out_hbm, out_w, out_sem)
    fetch_out.start()
    fetch_in = pltpu.make_async_copy(in_hbm, in_w, in_sem)
    fetch_in.start()
    pieces[me_tx] = att_ref[me_tx]
    greet(("tx", "ty"))
    deal(att_ref, pieces, a_send, a_recv, "tx")
    take_all(pieces, a_send, a_recv, "tx")
    block_rows, piece = pieces.shape[1], pieces.shape[2]
    own_rows = block_rows // count_tx
    for q in range(count_tx):
        blocks[me_ty, :, q * piece : (q + 1) * piece] = jnp.concatenate(
            [
                pieces[src].astype(jnp.float32)[q * own_rows : (q + 1) * own_rows]
                for src in range(count_tx)
            ],
            axis=0,
        ).astype(jnp.bfloat16)
    spread_own(blocks, b_send, b_recv, "ty")
    take_all(blocks, b_send, b_recv, "ty")
    fetch_out.wait()
    attended = blocks[...].reshape(rows, blocks.shape[2])
    for d in range(count_tx):
        part_out[d] = jnp.dot(
            attended, out_w[:, d * width : (d + 1) * width], preferred_element_type=jnp.float32
        ).astype(jnp.bfloat16)
    deal(part_out, part_in, p_send, p_recv, "tx")
    part_in[me_tx] = part_out[me_tx]
    take_all(part_in, p_send, p_recv, "tx")
    total = resid_ref[...].astype(jnp.float32)
    for src in range(count_tx):
        total = total + part_in[src].astype(jnp.float32)
    hidden = total.astype(jnp.bfloat16)
    hidden_ref[...] = hidden
    gathered[me_tx, :rows, :] = hidden
    gathered[me_tx, rows:, :] = gain_ref[...]
    spread_own(gathered, g_send, g_recv, "tx")
    take_all(gathered, g_send, g_recv, "tx")
    square = gained_rows(gathered, rows, scaled)
    fetch_in.wait()
    start = jnp.dot(scaled[...], in_w[...], preferred_element_type=jnp.float32)
    message = jnp.concatenate([start.astype(jnp.bfloat16), split_square(square)], axis=1)
    slots = slots_out.shape[1]
    for owner in range(count_ty):
        slots_out[owner] = jnp.dot(
            select_ref[owner * slots : (owner + 1) * slots, :],
            message,
            preferred_element_type=jnp.float32,
        ).astype(jnp.bfloat16)
    deal(slots_out, slots_in, s_send, s_recv, "ty")
    slots_in[me_ty] = slots_out[me_ty]
    take_all(slots_in, s_send, s_recv, "ty")
    part_width = start.shape[1]
    total = jnp.zeros((slots, part_width), jnp.float32)
    square = jnp.zeros((slots, 1), jnp.float32)
    for src in range(count_ty):
        total = total + slots_in[src, :, :part_width].astype(jnp.float32)
        square = square + join_square(slots_in[src, :, part_width:])
    state_ref[...] = (
        (total * lax.rsqrt(square / full_width + epsilon)).astype(jnp.bfloat16).astype(jnp.float32)
    )
    settle(pieces, a_send, a_recv, "tx")
    settle(blocks, b_send, b_recv, "ty")
    settle(part_in, p_send, p_recv, "tx")
    settle(gathered, g_send, g_recv, "tx")
    settle(slots_in, s_send, s_recv, "ty")


def out_rows(
    attended, out_weight, residual, gain, in_weight, select, full_width, slots, count_tx, count_ty
):
    rows, width = residual.shape
    block_rows = attended.shape[1]
    columns = in_weight.shape[1]
    dma = pltpu.SemaphoreType.DMA
    inside = pl.BlockSpec(memory_space=pltpu.VMEM)
    outside = pl.BlockSpec(memory_space=pl.ANY)
    return pl.pallas_call(
        functools.partial(out_kernel, full_width),
        out_shape=(
            jax.ShapeDtypeStruct((rows, width), jnp.bfloat16),
            jax.ShapeDtypeStruct((slots, columns), jnp.float32),
        ),
        in_specs=[inside, outside, inside, inside, outside, inside],
        out_specs=(inside, inside),
        scratch_shapes=[
            pltpu.VMEM(out_weight.shape, jnp.bfloat16),
            pltpu.VMEM(in_weight.shape, jnp.bfloat16),
            pltpu.VMEM(attended.shape, jnp.bfloat16),
            pltpu.VMEM((count_ty, block_rows, out_weight.shape[0]), jnp.bfloat16),
            pltpu.VMEM((count_tx, rows, width), jnp.bfloat16),
            pltpu.VMEM((count_tx, rows, width), jnp.bfloat16),
            pltpu.VMEM((count_tx, rows + PAD, width), jnp.bfloat16),
            pltpu.VMEM((rows, count_tx * width), jnp.bfloat16),
            pltpu.VMEM((count_ty, slots, columns + LANES), jnp.bfloat16),
            pltpu.VMEM((count_ty, slots, columns + LANES), jnp.bfloat16),
            dma, dma,
            dma((count_tx,)), dma((count_tx,)),
            dma((count_ty,)), dma((count_ty,)),
            dma((count_tx,)), dma((count_tx,)),
            dma((count_tx,)), dma((count_tx,)),
            dma((count_ty,)), dma((count_ty,)),
        ],
        compiler_params=pltpu.CompilerParams(
            collective_id=2, has_side_effects=True, vmem_limit_bytes=VMEM_BYTES
        ),
    )(attended, out_weight, residual, gain, in_weight, select)


def depth_kernel(
    start_ref, codes_ref, pre_ref, head_ref, gate_hbm, up_hbm, down_hbm, table_hbm, out_ref,
    gate, up, down, table, state, gate_sum, up_sum, pre, out, sums_out, sums_in, words_out,
    words_in, ends, w_sem, pre_s, pre_r, out_s, out_r, sum_s, sum_r, word_s, word_r, end_s, end_r,
):
    me, count = lax.axis_index("tx"), lax.axis_size("tx")
    slots, width = start_ref.shape
    entries = table.shape[1]
    full = width * count
    fetches = [
        pltpu.make_async_copy(far, near, w_sem.at[i])
        for i, (far, near) in enumerate(
            ((gate_hbm, gate), (up_hbm, up), (down_hbm, down), (table_hbm, table))
        )
    ]
    for fetch in fetches:
        fetch.start()
    state[...] = start_ref[...]
    ends[me] = jnp.zeros(ends.shape[1:], jnp.float32)
    greet(("tx",))
    for fetch in fetches:
        fetch.wait()
    lane = lax.broadcasted_iota(jnp.int32, (slots, LANES), 1)
    entry = lax.broadcasted_iota(jnp.int32, (slots, entries), 1)

    def chosen(k):
        return codes_ref[k] - me * entries == entry

    def announce(buffer, k, gain_ref, send_sems, recv_sems):
        values = state[...]
        buffer[k, me, :, :width] = (values * gain_ref[...].astype(jnp.float32)).astype(jnp.bfloat16)
        buffer[k, me, :, width:] = split_square(jnp.sum(values * values, axis=1, keepdims=True))
        spread_own(buffer.at[k], send_sems.at[k], recv_sems.at[k], "tx")

    def score(k):
        logits = jnp.zeros((slots, entries), jnp.float32)
        square = jnp.zeros((slots, 1), jnp.float32)
        for step in range(count):
            if step:
                take(out.at[k], out_s.at[k], out_r.at[k], "tx", step)
            src = lax.rem(me + count - step, count)
            columns = pl.ds(pl.multiple_of(src * width, width), width)
            logits = logits + lax.dot_general(
                out[k, src, :, :width],
                table[k, :, columns],
                (((1,), (1,)), ((), ())),
                preferred_element_type=jnp.float32,
            )
            square = square + join_square(out[k, src, :, width:])
        logits = logits * lax.rsqrt(square / full + epsilon)
        total = jnp.sum(jnp.exp(logits), axis=1, keepdims=True)
        picked = jnp.sum(jnp.where(chosen(k), logits, 0.0), axis=1, keepdims=True)
        ends[me, 0] = jnp.where(lane == k, total, ends[me, 0])
        ends[me, 1] = jnp.where(lane == k, picked, ends[me, 1])

    def one_step(k, carry):
        announce(pre, k, pre_ref, pre_s, pre_r)

        @pl.when(k < STEPS - 1)
        def _():
            found = chosen(k).astype(jnp.float32).astype(jnp.bfloat16)
            for d in range(count):
                words_out[k, d] = jnp.dot(
                    found, table[k, :, d * width : (d + 1) * width],
                    preferred_element_type=jnp.float32,
                ).astype(jnp.bfloat16)
            deal(words_out.at[k], words_in.at[k], word_s.at[k], word_r.at[k], "tx")
            words_in[k, me] = words_out[k, me]

        square = jnp.zeros((slots, 1), jnp.float32)
        for step in range(count):
            if step:
                take(pre.at[k], pre_s.at[k], pre_r.at[k], "tx", step)
            src = lax.rem(me + count - step, count)
            depth = pl.ds(pl.multiple_of(src * width, width), width)
            block = pre[k, src, :, :width]
            gate_part = jnp.dot(block, gate[depth, :], preferred_element_type=jnp.float32)
            up_part = jnp.dot(block, up[depth, :], preferred_element_type=jnp.float32)
            if step:
                gate_part = gate_sum[...] + gate_part
                up_part = up_sum[...] + up_part
            gate_sum[...] = gate_part
            up_sum[...] = up_part
            square = square + join_square(pre[k, src, :, width:])
        scale = lax.rsqrt(square / full + epsilon)
        gate_part = gate_sum[...] * scale
        act = (gate_part / (1.0 + jnp.exp(-gate_part)) * (up_sum[...] * scale)).astype(jnp.bfloat16)
        for step in range(count - 1, -1, -1):
            peer = lax.rem(me + step, count)
            columns = pl.ds(pl.multiple_of(peer * width, width), width)
            part = jnp.dot(act, down[:, columns], preferred_element_type=jnp.float32)
            if step:
                sums_out[k, peer] = part.astype(jnp.bfloat16)
                push(
                    sums_out.at[k, peer], sums_in.at[k, me], sum_s.at[k, peer], sum_r.at[k, me],
                    "tx", peer,
                ).start()
            else:
                state[...] = state[...] + part

        @pl.when(k > 0)
        def _():
            score(k - 1)

        total = jnp.zeros((slots, width), jnp.float32)
        for step in range(1, count):
            src = take(sums_in.at[k], sum_s.at[k], sum_r.at[k], "tx", step)
            total = total + sums_in[k, src].astype(jnp.float32)
        state[...] = state[...] + total
        announce(out, k, head_ref, out_s, out_r)

        @pl.when(k < STEPS - 1)
        def _():
            word = words_in[k, me].astype(jnp.float32)
            for step in range(1, count):
                src = take(words_in.at[k], word_s.at[k], word_r.at[k], "tx", step)
                word = word + words_in[k, src].astype(jnp.float32)
            state[...] = state[...] + embed_gain * word

        return carry

    lax.fori_loop(0, STEPS, one_step, 0)
    score(STEPS - 1)
    spread_own(ends, end_s, end_r, "tx")
    take_all(ends, end_s, end_r, "tx")
    total = ends[0, 0]
    picked = ends[0, 1]
    for src in range(1, count):
        total = total + ends[src, 0]
        picked = picked + ends[src, 1]
    out_ref[...] = picked - jnp.log(jnp.where(lane < STEPS, total, 1.0))

    def close(k, carry):
        settle(pre.at[k], pre_s.at[k], pre_r.at[k], "tx")
        settle(out.at[k], out_s.at[k], out_r.at[k], "tx")
        settle(sums_in.at[k], sum_s.at[k], sum_r.at[k], "tx")

        @pl.when(k < STEPS - 1)
        def _():
            settle(words_in.at[k], word_s.at[k], word_r.at[k], "tx")

        return carry

    lax.fori_loop(0, STEPS, close, 0)
    settle(ends, end_s, end_r, "tx")


def depth_rows(start, codes, pre_gain, head_gain, mlp_gate, mlp_up, mlp_down, table, count_tx):
    slots, width = start.shape
    dma = pltpu.SemaphoreType.DMA
    inside = pl.BlockSpec(memory_space=pltpu.VMEM)
    outside = pl.BlockSpec(memory_space=pl.ANY)
    bf16, f32 = jnp.bfloat16, jnp.float32
    each = (STEPS, count_tx)
    return pl.pallas_call(
        depth_kernel,
        out_shape=jax.ShapeDtypeStruct((slots, LANES), f32),
        in_specs=[inside] * 4 + [outside] * 4,
        out_specs=inside,
        scratch_shapes=[
            pltpu.VMEM(mlp_gate.shape, bf16),
            pltpu.VMEM(mlp_up.shape, bf16),
            pltpu.VMEM(mlp_down.shape, bf16),
            pltpu.VMEM(table.shape, bf16),
            pltpu.VMEM((slots, width), f32),
            pltpu.VMEM((slots, mlp_gate.shape[1]), f32),
            pltpu.VMEM((slots, mlp_gate.shape[1]), f32),
            pltpu.VMEM(each + (slots, width + LANES), bf16),
            pltpu.VMEM(each + (slots, width + LANES), bf16),
            pltpu.VMEM(each + (slots, width), bf16),
            pltpu.VMEM(each + (slots, width), bf16),
            pltpu.VMEM(each + (slots, width), bf16),
            pltpu.VMEM(each + (slots, width), bf16),
            pltpu.VMEM((count_tx, 2, slots, LANES), f32),
            dma((4,)),
            dma(each), dma(each), dma(each), dma(each),
            dma(each), dma(each), dma(each), dma(each),
            dma((count_tx,)), dma((count_tx,)),
        ],
        compiler_params=pltpu.CompilerParams(
            collective_id=3, has_side_effects=True, vmem_limit_bytes=VMEM_BYTES
        ),
    )(start, codes, pre_gain, head_gain, mlp_gate, mlp_up, mlp_down, table)


def padded_gain(gain):
    return jnp.pad(gain[None, :], ((0, PAD - 1), (0, 0)))


def body(
    hidden_in,
    norm_gain,
    qkv_weight,
    qkv_bias,
    key_cache,
    value_cache,
    lengths,
    out_weight,
    final_gain,
    in_weight,
    owners,
    codebook_ids,
    mlp_gate,
    mlp_up,
    mlp_down,
    pre_gain,
    head_gain,
    codebook_table,
):
    count_tx = lax.axis_size("tx")
    count_ty = lax.axis_size("ty")
    batch_rows = hidden_in.shape[0]
    own_rows = key_cache.shape[0]
    block_rows = batch_rows // count_ty
    full_width = hidden_in.shape[1] * count_tx * count_ty
    entry = jnp.concatenate([hidden_in, padded_gain(norm_gain)], axis=0)
    raw = qkv_rows(entry, qkv_weight, batch_rows, full_width, count_tx, count_ty)
    qkv_raw = (
        raw.reshape(count_tx, count_tx, own_rows, raw.shape[2])
        .transpose(2, 0, 1, 3)
        .reshape(own_rows, count_tx * count_tx * raw.shape[2])
    )
    qkv = qkv_raw.astype(jnp.float32) + qkv_bias.astype(jnp.float32)
    query_width = HEADS * HEAD_DIM
    key_width = KV_HEADS * HEAD_DIM
    query_heads = rotate(qkv[:, :query_width].reshape(own_rows, HEADS, HEAD_DIM), lengths)
    query_heads = (query_heads * HEAD_DIM ** (-0.5)).astype(jnp.bfloat16)
    new_key = rotate(
        qkv[:, query_width : query_width + key_width].reshape(own_rows, KV_HEADS, HEAD_DIM), lengths
    ).astype(jnp.bfloat16)
    new_value = (
        qkv[:, query_width + key_width :].reshape(own_rows, KV_HEADS, HEAD_DIM).astype(jnp.bfloat16)
    )
    attended = attend(query_heads, new_key, new_value, key_cache, value_cache, lengths)
    attended = (
        attended.reshape(own_rows, count_tx, count_tx, -1)
        .transpose(1, 2, 0, 3)
        .reshape(count_tx, count_tx * own_rows, -1)
    )
    capacity = max(2, 2 * own_rows * count_tx // count_ty)
    slot_count = count_ty * capacity
    earlier = jnp.arange(block_rows)[:, None] > jnp.arange(block_rows)[None, :]
    same = owners.reshape(count_ty, block_rows, 1) == owners.reshape(count_ty, 1, block_rows)
    rank = jnp.sum((same & earlier[None]).astype(jnp.int32), axis=2)
    slot = (jnp.arange(count_ty, dtype=jnp.int32)[:, None] * capacity + rank).reshape(-1)
    place = owners * slot_count + slot
    select = (
        place[None, :] == jnp.arange(count_ty * slot_count, dtype=jnp.int32)[:, None]
    ).astype(jnp.bfloat16)
    hidden_out, start = out_rows(
        attended,
        out_weight,
        hidden_in,
        padded_gain(final_gain),
        in_weight,
        select,
        full_width,
        slot_count,
        count_tx,
        count_ty,
    )
    my_owner = lax.axis_index("ty")
    mine = place[None, :] == my_owner * slot_count + jnp.arange(slot_count, dtype=jnp.int32)[:, None]
    filled = jnp.any(mine, axis=1)
    codes = jnp.sum(jnp.where(mine[:, :, None], codebook_ids[None], 0), axis=1)
    codes = jnp.where(filled[:, None], codes, -1)
    width = start.shape[1]
    offset = lax.axis_index("tx") * width
    logprob = depth_rows(
        start,
        codes.T[:, :, None],
        lax.dynamic_slice_in_dim(pre_gain, offset, width)[None],
        lax.dynamic_slice_in_dim(head_gain, offset, width)[None],
        mlp_gate,
        mlp_up,
        mlp_down,
        codebook_table,
        count_tx,
    )
    logprob = jnp.where(filled[:, None], logprob[:, :STEPS], 0.0)
    return (hidden_out, logprob.T[None])


def solution(mesh):
    placed = (
        P(None, ("ty", "tx")),
        P(("ty", "tx")),
        P("ty", "tx"),
        P(),
        P(("ty", "tx"), None, None),
        P(("ty", "tx"), None, None),
        P(("ty", "tx")),
        P("tx", "ty"),
        P(("ty", "tx")),
        P("ty", "tx"),
        P(),
        P(),
        P(None, "tx"),
        P(None, "tx"),
        P("tx", None),
        P(),
        P(),
        P(None, "tx", None),
    )
    return jax.shard_map(
        body,
        mesh=mesh,
        in_specs=placed,
        out_specs=(P(None, ("ty", "tx")), P("ty", None, None)),
        check_vma=False,
    )
```

```python
import functools

import jax
import jax.numpy as jnp
from jax import lax
from jax.experimental import pallas as pl
from jax.experimental.pallas import tpu as pltpu
from jax.sharding import PartitionSpec as P

HEADS = 64
KV_HEADS = 8
HEAD_DIM = 128
STEPS = 8
LMAX = 128
LANES = 128
PAD = 16
EARLY = 4
VMEM_BYTES = 56 * 1024 * 1024
MESH = pl.DeviceIdType.MESH

epsilon = 1e-06
rope_base = 1000000.0
embed_gain = 16.0


def rotate(values, position):
    half_dim = values.shape[-1] // 2
    frequency = jnp.exp(
        -jnp.log(rope_base) * (2.0 * jnp.arange(half_dim, dtype=jnp.float32) / values.shape[-1])
    )
    phase_angle = position.astype(jnp.float32)[:, None, None] * frequency[None, None, :]
    cosine = jnp.cos(phase_angle)
    sine_part = jnp.sin(phase_angle)
    first_half = values[..., :half_dim]
    second_half = values[..., half_dim:]
    return jnp.concatenate(
        [
            first_half * cosine - second_half * sine_part,
            second_half * cosine + first_half * sine_part,
        ],
        axis=-1,
    )


def attend(query_heads, new_key, new_value, key_cache, value_cache, lengths):
    row_count = query_heads.shape[0]
    group_size = HEADS // KV_HEADS
    query_heads = query_heads.reshape(row_count, KV_HEADS, group_size, HEAD_DIM)
    keys_all = key_cache.reshape(row_count, LMAX, KV_HEADS, HEAD_DIM)
    values_all = value_cache.reshape(row_count, LMAX, KV_HEADS, HEAD_DIM)
    scores = jnp.einsum(
        "rgjd,rtgd->rgjt", query_heads, keys_all, preferred_element_type=jnp.float32
    )
    own_score = jnp.einsum(
        "rgjd,rgd->rgj", query_heads, new_key, preferred_element_type=jnp.float32
    )
    in_cache = jnp.arange(LMAX, dtype=jnp.int32)[None, :] < lengths[:, None]
    weights = jnp.where(in_cache[:, None, None, :], jnp.exp(scores), 0.0)
    own_weight = jnp.exp(own_score)
    denominator = jnp.sum(weights, axis=-1) + own_weight
    probability = (weights / denominator[..., None]).astype(jnp.bfloat16)
    own_prob = (own_weight / denominator).astype(jnp.bfloat16)
    blended = jnp.einsum(
        "rgjt,rtgd->rgjd", probability, values_all, preferred_element_type=jnp.float32
    )
    blended = (
        blended
        + own_prob.astype(jnp.float32)[..., None] * new_value.astype(jnp.float32)[:, :, None, :]
    )
    return blended.reshape(row_count, HEADS * HEAD_DIM).astype(jnp.bfloat16)


def split_square(total):
    total = jnp.broadcast_to(total, (total.shape[0], LANES))
    high = total.astype(jnp.bfloat16)
    low = (total - high.astype(jnp.float32)).astype(jnp.bfloat16)
    lane = lax.broadcasted_iota(jnp.int32, total.shape, 1)
    return jnp.where(lane < LANES // 2, high.astype(jnp.float32), low.astype(jnp.float32)).astype(
        jnp.bfloat16
    )


def join_square(block):
    block = block.astype(jnp.float32)
    return block[:, :1] + block[:, LANES // 2 : LANES // 2 + 1]


def push(source, target, send_sem, recv_sem, axis, peer):
    return pltpu.make_async_remote_copy(
        src_ref=source,
        dst_ref=target,
        send_sem=send_sem,
        recv_sem=recv_sem,
        device_id={axis: peer},
        device_id_type=MESH,
    )


def greet(axes):
    barrier = pltpu.get_barrier_semaphore()
    count = 0
    for axis in axes:
        me, size = lax.axis_index(axis), lax.axis_size(axis)
        for step in range(1, size):
            pl.semaphore_signal(
                barrier,
                inc=1,
                device_id={axis: lax.rem(me + step, size)},
                device_id_type=MESH,
            )
        count += size - 1
    pl.semaphore_wait(barrier, count)


def spread_own(buffer, send_sems, recv_sems, axis):
    me, size = lax.axis_index(axis), lax.axis_size(axis)
    for step in range(1, size):
        peer = lax.rem(me + step, size)
        push(
            buffer.at[me], buffer.at[me], send_sems.at[peer], recv_sems.at[me], axis, peer
        ).start()


def deal(source, buffer, send_sems, recv_sems, axis):
    me, size = lax.axis_index(axis), lax.axis_size(axis)
    for step in range(1, size):
        peer = lax.rem(me + step, size)
        push(
            source.at[peer], buffer.at[me], send_sems.at[peer], recv_sems.at[me], axis, peer
        ).start()


def take(buffer, send_sems, recv_sems, axis, step):
    me, size = lax.axis_index(axis), lax.axis_size(axis)
    peer = lax.rem(me + size - step, size)
    push(buffer.at[peer], buffer.at[peer], send_sems.at[peer], recv_sems.at[peer], axis, peer).wait_recv()
    return peer


def take_all(buffer, send_sems, recv_sems, axis):
    for step in range(1, lax.axis_size(axis)):
        take(buffer, send_sems, recv_sems, axis, step)


def settle(buffer, send_sems, recv_sems, axis):
    me, size = lax.axis_index(axis), lax.axis_size(axis)
    for step in range(1, size):
        peer = lax.rem(me + step, size)
        push(buffer.at[peer], buffer.at[peer], send_sems.at[peer], recv_sems.at[me], axis, peer).wait_send()


def gained_rows(blocks, rows, scaled_ref):
    square = jnp.zeros((rows, 1), jnp.float32)
    width = blocks.shape[2]
    for part in range(blocks.shape[0]):
        values = blocks[part, :rows, :].astype(jnp.float32)
        gain = blocks[part, rows : rows + PAD, :].astype(jnp.float32)[:1]
        square = square + jnp.sum(values * values, axis=1, keepdims=True)
        scaled_ref[:, part * width : (part + 1) * width] = (values * gain).astype(jnp.bfloat16)
    return square


def qkv_kernel(
    full_width, entry_ref, weight_hbm, out_ref, weight, gathered, scaled, sums_out, sums_in,
    rows_out, rows_in, weight_sem, g_send, g_recv, s_send, s_recv, r_send, r_recv,
):
    me_tx, me_ty = lax.axis_index("tx"), lax.axis_index("ty")
    count_tx, count_ty = lax.axis_size("tx"), lax.axis_size("ty")
    rows = scaled.shape[0]
    columns = weight.shape[1]
    fetch = pltpu.make_async_copy(weight_hbm, weight, weight_sem)
    fetch.start()
    gathered[me_tx] = entry_ref[...]
    greet(("tx", "ty"))
    spread_own(gathered, g_send, g_recv, "tx")
    take_all(gathered, g_send, g_recv, "tx")
    square = gained_rows(gathered, rows, scaled)
    fetch.wait()
    tile = 512
    block_rows = rows // count_ty
    for start in range(0, columns, tile):
        part = jnp.dot(
            scaled[...], weight[:, start : start + tile], preferred_element_type=jnp.float32
        )
        sums_out[:, :, start : start + tile] = part.astype(jnp.bfloat16).reshape(
            count_ty, block_rows, tile
        )
    sums_out[:, :, columns:] = split_square(square).reshape(count_ty, block_rows, LANES)
    deal(sums_out, sums_in, s_send, s_recv, "ty")
    sums_in[me_ty] = sums_out[me_ty]
    take_all(sums_in, s_send, s_recv, "ty")
    square = jnp.zeros((block_rows, 1), jnp.float32)
    for part in range(count_ty):
        square = square + join_square(sums_in[part, :, columns:])
    scale = lax.rsqrt(square / full_width + epsilon)
    own_rows = block_rows // count_tx
    piece = columns // count_tx
    raw = []
    for q in range(count_tx):
        total = jnp.zeros((block_rows, piece), jnp.float32)
        for part in range(count_ty):
            total = total + sums_in[part, :, q * piece : (q + 1) * piece].astype(jnp.float32)
        raw.append(total * scale)
    for d in range(count_tx):
        rows_out[d] = jnp.concatenate(
            [part[d * own_rows : (d + 1) * own_rows] for part in raw], axis=0
        ).astype(jnp.bfloat16)
    deal(rows_out, rows_in, r_send, r_recv, "tx")
    rows_in[me_tx] = rows_out[me_tx]
    take_all(rows_in, r_send, r_recv, "tx")
    out_ref[...] = rows_in[...]
    settle(gathered, g_send, g_recv, "tx")
    settle(sums_in, s_send, s_recv, "ty")
    settle(rows_in, r_send, r_recv, "tx")


def qkv_rows(entry, qkv_weight, rows, full_width, count_tx, count_ty):
    columns = qkv_weight.shape[1]
    block_rows = rows // count_ty
    piece = columns // count_tx
    dma = pltpu.SemaphoreType.DMA
    return pl.pallas_call(
        functools.partial(qkv_kernel, full_width),
        out_shape=jax.ShapeDtypeStruct((count_tx, block_rows, piece), jnp.bfloat16),
        in_specs=[
            pl.BlockSpec(memory_space=pltpu.VMEM),
            pl.BlockSpec(memory_space=pl.ANY),
        ],
        out_specs=pl.BlockSpec(memory_space=pltpu.VMEM),
        scratch_shapes=[
            pltpu.VMEM(qkv_weight.shape, jnp.bfloat16),
            pltpu.VMEM((count_tx,) + entry.shape, jnp.bfloat16),
            pltpu.VMEM((rows, count_tx * entry.shape[1]), jnp.bfloat16),
            pltpu.VMEM((count_ty, block_rows, columns + LANES), jnp.bfloat16),
            pltpu.VMEM((count_ty, block_rows, columns + LANES), jnp.bfloat16),
            pltpu.VMEM((count_tx, block_rows, piece), jnp.bfloat16),
            pltpu.VMEM((count_tx, block_rows, piece), jnp.bfloat16),
            dma,
            dma((count_tx,)), dma((count_tx,)),
            dma((count_ty,)), dma((count_ty,)),
            dma((count_tx,)), dma((count_tx,)),
        ],
        compiler_params=pltpu.CompilerParams(
            collective_id=1, has_side_effects=True, vmem_limit_bytes=VMEM_BYTES
        ),
    )(entry, qkv_weight)


def tail_kernel(
    full_width, att_ref, out_hbm, resid_ref, gain_ref, in_hbm, codes_ref, gains_ref, gate_hbm,
    up_hbm, down_hbm, table_hbm, hidden_ref, out_ref,
    out_w, in_w, gate, up, down, table, pieces, blocks, part_out, part_in, gathered, scaled,
    starts_out, starts_in, state, gate_sum, up_sum, pre, out, sums_out, sums_in, words_out,
    words_in, ends, finals,
    w_sem, a_send, a_recv, b_send, b_recv, p_send, p_recv, g_send, g_recv, s_send, s_recv,
    pre_s, pre_r, out_s, out_r, sum_s, sum_r, word_s, word_r, end_s, end_r, fin_s, fin_r,
):
    me, me_ty = lax.axis_index("tx"), lax.axis_index("ty")
    count, count_ty = lax.axis_size("tx"), lax.axis_size("ty")
    rows, feature_width = resid_ref.shape
    block_rows, width = state.shape
    entries = table.shape[1]
    full = width * count
    fetch_out, fetch_table, fetch_in, *fetch_rest = [
        pltpu.make_async_copy(far, near, w_sem.at[i])
        for i, (far, near) in enumerate(
            (
                (out_hbm, out_w),
                (table_hbm, table),
                (in_hbm, in_w),
                (gate_hbm, gate),
                (up_hbm, up),
                (down_hbm, down),
            )
        )
    ]
    for fetch in [fetch_out, fetch_table, fetch_in] + fetch_rest:
        fetch.start()
    lane = lax.broadcasted_iota(jnp.int32, (block_rows, LANES), 1)
    entry = lax.broadcasted_iota(jnp.int32, (block_rows, entries), 1)
    codes = codes_ref[me_ty]
    code_lane = lax.broadcasted_iota(jnp.int32, codes.shape, 1)

    def chosen(k):
        code = jnp.sum(jnp.where(code_lane == k, codes, 0), axis=1, keepdims=True)
        return code - me * entries == entry

    def send_words(k):
        found = chosen(k).astype(jnp.float32).astype(jnp.bfloat16)
        for d in range(count):
            words_out[k, d] = jnp.dot(
                found, table[k, :, d * width : (d + 1) * width], preferred_element_type=jnp.float32
            ).astype(jnp.bfloat16)
        deal(words_out.at[k], words_in.at[k], word_s.at[k], word_r.at[k], "tx")
        words_in[k, me] = words_out[k, me]

    pieces[me] = att_ref[me]
    greet(("tx", "ty"))
    deal(att_ref, pieces, a_send, a_recv, "tx")
    take_all(pieces, a_send, a_recv, "tx")
    piece = pieces.shape[2]
    own_rows = block_rows // count
    for q in range(count):
        blocks[me_ty, :, q * piece : (q + 1) * piece] = jnp.concatenate(
            [
                pieces[src].astype(jnp.float32)[q * own_rows : (q + 1) * own_rows]
                for src in range(count)
            ],
            axis=0,
        ).astype(jnp.bfloat16)
    spread_own(blocks, b_send, b_recv, "ty")
    fetch_table.wait()

    def early_words(k, carry):
        send_words(k)
        return carry

    lax.fori_loop(0, EARLY, early_words, 0)
    take_all(blocks, b_send, b_recv, "ty")
    fetch_out.wait()
    attended = blocks[...].reshape(rows, blocks.shape[2])
    for d in range(count):
        part_out[d] = jnp.dot(
            attended,
            out_w[:, d * feature_width : (d + 1) * feature_width],
            preferred_element_type=jnp.float32,
        ).astype(jnp.bfloat16)
    deal(part_out, part_in, p_send, p_recv, "tx")
    part_in[me] = part_out[me]
    take_all(part_in, p_send, p_recv, "tx")
    total = resid_ref[...].astype(jnp.float32)
    for src in range(count):
        total = total + part_in[src].astype(jnp.float32)
    hidden = total.astype(jnp.bfloat16)
    hidden_ref[...] = hidden
    gathered[me, :rows, :] = hidden
    gathered[me, rows:, :] = gain_ref[...]
    spread_own(gathered, g_send, g_recv, "tx")
    take_all(gathered, g_send, g_recv, "tx")
    square = gained_rows(gathered, rows, scaled)
    fetch_in.wait()
    start = jnp.dot(scaled[...], in_w[...], preferred_element_type=jnp.float32)
    starts_out[:, :, :width] = start.astype(jnp.bfloat16).reshape(count_ty, block_rows, width)
    starts_out[:, :, width:] = split_square(square).reshape(count_ty, block_rows, LANES)
    deal(starts_out, starts_in, s_send, s_recv, "ty")
    starts_in[me_ty] = starts_out[me_ty]
    ends[me] = jnp.zeros(ends.shape[1:], jnp.float32)
    for fetch in fetch_rest:
        fetch.wait()
    take_all(starts_in, s_send, s_recv, "ty")
    total = jnp.zeros((block_rows, width), jnp.float32)
    square = jnp.zeros((block_rows, 1), jnp.float32)
    for src in range(count_ty):
        total = total + starts_in[src, :, :width].astype(jnp.float32)
        square = square + join_square(starts_in[src, :, width:])
    scale = lax.rsqrt(square / full_width + epsilon)
    state[...] = (total * scale).astype(jnp.bfloat16).astype(jnp.float32)

    def announce(buffer, k, values, send_sems, recv_sems):
        buffer[k, me] = values.astype(jnp.bfloat16)
        spread_own(buffer.at[k], send_sems.at[k], recv_sems.at[k], "tx")

    def gained(buffer, k, src, which):
        values = buffer[k, src].astype(jnp.float32)
        square = jnp.sum(values * values, axis=1, keepdims=True)
        return (values * gains_ref[which, src]).astype(jnp.bfloat16), square

    def score(k):
        logits = jnp.zeros((block_rows, entries), jnp.float32)
        square = jnp.zeros((block_rows, 1), jnp.float32)
        for step in range(count):
            if step:
                take(out.at[k], out_s.at[k], out_r.at[k], "tx", step)
            src = lax.rem(me + count - step, count)
            columns = pl.ds(pl.multiple_of(src * width, width), width)
            block, term = gained(out, k, src, 1)
            logits = logits + lax.dot_general(
                block,
                table[k, :, columns],
                (((1,), (1,)), ((), ())),
                preferred_element_type=jnp.float32,
            )
            square = square + term
        logits = logits * lax.rsqrt(square / full + epsilon)
        total = jnp.sum(jnp.exp(logits), axis=1, keepdims=True)
        picked = jnp.sum(jnp.where(chosen(k), logits, 0.0), axis=1, keepdims=True)
        ends[me, 0] = jnp.where(lane == k, total, ends[me, 0])
        ends[me, 1] = jnp.where(lane == k, picked, ends[me, 1])

    def one_step(k, carry):
        @pl.when(k < STEPS - 1 - EARLY)
        def _():
            send_words(k + EARLY)

        square = jnp.zeros((block_rows, 1), jnp.float32)
        for step in range(count):
            if step:
                take(pre.at[k], pre_s.at[k], pre_r.at[k], "tx", step)
            src = lax.rem(me + count - step, count)
            depth = pl.ds(pl.multiple_of(src * width, width), width)
            block, term = gained(pre, k, src, 0)
            gate_part = jnp.dot(block, gate[depth, :], preferred_element_type=jnp.float32)
            up_part = jnp.dot(block, up[depth, :], preferred_element_type=jnp.float32)
            if step:
                gate_part = gate_sum[...] + gate_part
                up_part = up_sum[...] + up_part
            gate_sum[...] = gate_part
            up_sum[...] = up_part
            square = square + term
        scale = lax.rsqrt(square / full + epsilon)
        gate_part = gate_sum[...] * scale
        act = (gate_part / (1.0 + jnp.exp(-gate_part)) * (up_sum[...] * scale)).astype(jnp.bfloat16)
        for step in range(count - 1, -1, -1):
            peer = lax.rem(me + step, count)
            columns = pl.ds(pl.multiple_of(peer * width, width), width)
            part = jnp.dot(act, down[:, columns], preferred_element_type=jnp.float32)
            if step:
                sums_out[k, peer] = part.astype(jnp.bfloat16)
                push(
                    sums_out.at[k, peer], sums_in.at[k, me], sum_s.at[k, peer], sum_r.at[k, me],
                    "tx", peer,
                ).start()
            else:
                state[...] = state[...] + part

        @pl.when(k > 0)
        def _():
            score(k - 1)

        total = jnp.zeros((block_rows, width), jnp.float32)
        for step in range(1, count):
            src = take(sums_in.at[k], sum_s.at[k], sum_r.at[k], "tx", step)
            total = total + sums_in[k, src].astype(jnp.float32)
        settled = state[...] + total

        @pl.when(k < STEPS - 1)
        def _():
            word = words_in[k, me].astype(jnp.float32)
            for step in range(1, count):
                src = take(words_in.at[k], word_s.at[k], word_r.at[k], "tx", step)
                word = word + words_in[k, src].astype(jnp.float32)
            entering = settled + embed_gain * word
            state[...] = entering
            announce(pre, k + 1, entering, pre_s, pre_r)

        announce(out, k, settled, out_s, out_r)
        return carry

    announce(pre, 0, state[...], pre_s, pre_r)
    lax.fori_loop(0, STEPS, one_step, 0)
    score(STEPS - 1)
    spread_own(ends, end_s, end_r, "tx")
    take_all(ends, end_s, end_r, "tx")
    total = ends[0, 0]
    picked = ends[0, 1]
    for src in range(1, count):
        total = total + ends[src, 0]
        picked = picked + ends[src, 1]
    finals[me_ty] = picked - jnp.log(jnp.where(lane < STEPS, total, 1.0))
    spread_own(finals, fin_s, fin_r, "ty")
    take_all(finals, fin_s, fin_r, "ty")
    out_ref[...] = finals[...]
    settle(pieces, a_send, a_recv, "tx")
    settle(blocks, b_send, b_recv, "ty")
    settle(part_in, p_send, p_recv, "tx")
    settle(gathered, g_send, g_recv, "tx")
    settle(starts_in, s_send, s_recv, "ty")

    def close(k, carry):
        settle(pre.at[k], pre_s.at[k], pre_r.at[k], "tx")
        settle(out.at[k], out_s.at[k], out_r.at[k], "tx")
        settle(sums_in.at[k], sum_s.at[k], sum_r.at[k], "tx")

        @pl.when(k < STEPS - 1)
        def _():
            settle(words_in.at[k], word_s.at[k], word_r.at[k], "tx")

        return carry

    lax.fori_loop(0, STEPS, close, 0)
    settle(ends, end_s, end_r, "tx")
    settle(finals, fin_s, fin_r, "ty")


def tail_rows(
    attended, out_weight, residual, gain, in_weight, codes, gains, mlp_gate, mlp_up, mlp_down,
    table, full_width, count_tx, count_ty,
):
    rows, width = residual.shape
    block_rows = attended.shape[1]
    columns = in_weight.shape[1]
    hidden_units = mlp_gate.shape[1]
    dma = pltpu.SemaphoreType.DMA
    inside = pl.BlockSpec(memory_space=pltpu.VMEM)
    outside = pl.BlockSpec(memory_space=pl.ANY)
    bf16, f32 = jnp.bfloat16, jnp.float32
    each = (STEPS, count_tx)
    by_tx, by_ty = dma((count_tx,)), dma((count_ty,))
    return pl.pallas_call(
        functools.partial(tail_kernel, full_width),
        out_shape=(
            jax.ShapeDtypeStruct((rows, width), bf16),
            jax.ShapeDtypeStruct((count_ty, block_rows, LANES), f32),
        ),
        in_specs=[inside, outside, inside, inside, outside, inside, inside] + [outside] * 4,
        out_specs=(inside, inside),
        scratch_shapes=[
            pltpu.VMEM(out_weight.shape, bf16),
            pltpu.VMEM(in_weight.shape, bf16),
            pltpu.VMEM(mlp_gate.shape, bf16),
            pltpu.VMEM(mlp_up.shape, bf16),
            pltpu.VMEM(mlp_down.shape, bf16),
            pltpu.VMEM(table.shape, bf16),
            pltpu.VMEM(attended.shape, bf16),
            pltpu.VMEM((count_ty, block_rows, out_weight.shape[0]), bf16),
            pltpu.VMEM((count_tx, rows, width), bf16),
            pltpu.VMEM((count_tx, rows, width), bf16),
            pltpu.VMEM((count_tx, rows + PAD, width), bf16),
            pltpu.VMEM((rows, count_tx * width), bf16),
            pltpu.VMEM((count_ty, block_rows, columns + LANES), bf16),
            pltpu.VMEM((count_ty, block_rows, columns + LANES), bf16),
            pltpu.VMEM((block_rows, columns), f32),
            pltpu.VMEM((block_rows, hidden_units), f32),
            pltpu.VMEM((block_rows, hidden_units), f32),
        ]
        + [pltpu.VMEM(each + (block_rows, columns), bf16)] * 6
        + [
            pltpu.VMEM((count_tx, 2, block_rows, LANES), f32),
            pltpu.VMEM((count_ty, block_rows, LANES), f32),
            dma((6,)),
            by_tx, by_tx, by_ty, by_ty, by_tx, by_tx, by_tx, by_tx, by_ty, by_ty,
        ]
        + [dma(each)] * 8
        + [by_tx, by_tx, by_ty, by_ty],
        compiler_params=pltpu.CompilerParams(
            collective_id=2, has_side_effects=True, vmem_limit_bytes=VMEM_BYTES
        ),
    )(
        attended, out_weight, residual, gain, in_weight, codes, gains, mlp_gate, mlp_up, mlp_down,
        table,
    )


def padded_gain(gain):
    return jnp.pad(gain[None, :], ((0, PAD - 1), (0, 0)))


def body(
    hidden_in,
    norm_gain,
    qkv_weight,
    qkv_bias,
    key_cache,
    value_cache,
    lengths,
    out_weight,
    final_gain,
    in_weight,
    owners,
    codebook_ids,
    mlp_gate,
    mlp_up,
    mlp_down,
    pre_gain,
    head_gain,
    codebook_table,
):
    count_tx = lax.axis_size("tx")
    count_ty = lax.axis_size("ty")
    batch_rows = hidden_in.shape[0]
    own_rows = key_cache.shape[0]
    block_rows = batch_rows // count_ty
    full_width = hidden_in.shape[1] * count_tx * count_ty
    entry = jnp.concatenate([hidden_in, padded_gain(norm_gain)], axis=0)
    raw = qkv_rows(entry, qkv_weight, batch_rows, full_width, count_tx, count_ty)
    qkv_raw = (
        raw.reshape(count_tx, count_tx, own_rows, raw.shape[2])
        .transpose(2, 0, 1, 3)
        .reshape(own_rows, count_tx * count_tx * raw.shape[2])
    )
    qkv = qkv_raw.astype(jnp.float32) + qkv_bias.astype(jnp.float32)
    query_width = HEADS * HEAD_DIM
    key_width = KV_HEADS * HEAD_DIM
    query_heads = rotate(qkv[:, :query_width].reshape(own_rows, HEADS, HEAD_DIM), lengths)
    query_heads = (query_heads * HEAD_DIM ** (-0.5)).astype(jnp.bfloat16)
    new_key = rotate(
        qkv[:, query_width : query_width + key_width].reshape(own_rows, KV_HEADS, HEAD_DIM), lengths
    ).astype(jnp.bfloat16)
    new_value = (
        qkv[:, query_width + key_width :].reshape(own_rows, KV_HEADS, HEAD_DIM).astype(jnp.bfloat16)
    )
    attended = attend(query_heads, new_key, new_value, key_cache, value_cache, lengths)
    attended = (
        attended.reshape(own_rows, count_tx, count_tx, -1)
        .transpose(1, 2, 0, 3)
        .reshape(count_tx, count_tx * own_rows, -1)
    )
    width = in_weight.shape[1]
    gains = jnp.stack([pre_gain, head_gain]).astype(jnp.float32)
    hidden_out, logprob = tail_rows(
        attended,
        out_weight,
        hidden_in,
        padded_gain(final_gain),
        in_weight,
        codebook_ids.reshape(count_ty, block_rows, STEPS),
        gains.reshape(2, count_tx, 1, width),
        mlp_gate,
        mlp_up,
        mlp_down,
        codebook_table,
        full_width,
        count_tx,
        count_ty,
    )
    capacity = max(2, 2 * own_rows * count_tx // count_ty)
    slot_count = count_ty * capacity
    earlier = jnp.arange(block_rows)[:, None] > jnp.arange(block_rows)[None, :]
    same = owners.reshape(count_ty, block_rows, 1) == owners.reshape(count_ty, 1, block_rows)
    rank = jnp.sum((same & earlier[None]).astype(jnp.int32), axis=2)
    slot = (jnp.arange(count_ty, dtype=jnp.int32)[:, None] * capacity + rank).reshape(-1)
    place = jnp.where(owners == lax.axis_index("ty"), slot, -1)
    mine = place[None, :] == jnp.arange(slot_count, dtype=jnp.int32)[:, None]
    logprob = logprob.reshape(batch_rows, LANES)[:, :STEPS].T
    placed_rows = jnp.sum(jnp.where(mine[None], logprob[:, None, :], 0.0), axis=2)
    return (hidden_out, placed_rows[None])


def solution(mesh):
    placed = (
        P(None, ("ty", "tx")),
        P(("ty", "tx")),
        P("ty", "tx"),
        P(),
        P(("ty", "tx"), None, None),
        P(("ty", "tx"), None, None),
        P(("ty", "tx")),
        P("tx", "ty"),
        P(("ty", "tx")),
        P("ty", "tx"),
        P(),
        P(),
        P(None, "tx"),
        P(None, "tx"),
        P("tx", None),
        P(),
        P(),
        P(None, "tx", None),
    )
    return jax.shard_map(
        body,
        mesh=mesh,
        in_specs=placed,
        out_specs=(P(None, ("ty", "tx")), P("ty", None, None)),
        check_vma=False,
    )
```

```python
import functools

import jax
import jax.numpy as jnp
from jax import lax
from jax.experimental import pallas as pl
from jax.experimental.pallas import tpu as pltpu
from jax.sharding import PartitionSpec as P

HEADS = 64
KV_HEADS = 8
HEAD_DIM = 128
STEPS = 8
LMAX = 128
LANES = 128
PAD = 16
VMEM_BYTES = 56 * 1024 * 1024
MESH = pl.DeviceIdType.MESH

epsilon = 1e-06
rope_base = 1000000.0
embed_gain = 16.0


def rotate(values, position):
    half_dim = values.shape[-1] // 2
    frequency = jnp.exp(
        -jnp.log(rope_base) * (2.0 * jnp.arange(half_dim, dtype=jnp.float32) / values.shape[-1])
    )
    phase_angle = position.astype(jnp.float32)[:, None, None] * frequency[None, None, :]
    cosine = jnp.cos(phase_angle)
    sine_part = jnp.sin(phase_angle)
    first_half = values[..., :half_dim]
    second_half = values[..., half_dim:]
    return jnp.concatenate(
        [
            first_half * cosine - second_half * sine_part,
            second_half * cosine + first_half * sine_part,
        ],
        axis=-1,
    )


def attend(query_heads, new_key, new_value, key_cache, value_cache, lengths):
    row_count = query_heads.shape[0]
    group_size = HEADS // KV_HEADS
    query_heads = query_heads.reshape(row_count, KV_HEADS, group_size, HEAD_DIM)
    keys_all = key_cache.reshape(row_count, LMAX, KV_HEADS, HEAD_DIM)
    values_all = value_cache.reshape(row_count, LMAX, KV_HEADS, HEAD_DIM)
    scores = jnp.einsum(
        "rgjd,rtgd->rgjt", query_heads, keys_all, preferred_element_type=jnp.float32
    )
    own_score = jnp.einsum(
        "rgjd,rgd->rgj", query_heads, new_key, preferred_element_type=jnp.float32
    )
    in_cache = jnp.arange(LMAX, dtype=jnp.int32)[None, :] < lengths[:, None]
    weights = jnp.where(in_cache[:, None, None, :], jnp.exp(scores), 0.0)
    own_weight = jnp.exp(own_score)
    denominator = jnp.sum(weights, axis=-1) + own_weight
    probability = (weights / denominator[..., None]).astype(jnp.bfloat16)
    own_prob = (own_weight / denominator).astype(jnp.bfloat16)
    blended = jnp.einsum(
        "rgjt,rtgd->rgjd", probability, values_all, preferred_element_type=jnp.float32
    )
    blended = (
        blended
        + own_prob.astype(jnp.float32)[..., None] * new_value.astype(jnp.float32)[:, :, None, :]
    )
    return blended.reshape(row_count, HEADS * HEAD_DIM).astype(jnp.bfloat16)


def split_square(total):
    total = jnp.broadcast_to(total, (total.shape[0], LANES))
    high = total.astype(jnp.bfloat16)
    low = (total - high.astype(jnp.float32)).astype(jnp.bfloat16)
    lane = lax.broadcasted_iota(jnp.int32, total.shape, 1)
    return jnp.where(lane < LANES // 2, high.astype(jnp.float32), low.astype(jnp.float32)).astype(
        jnp.bfloat16
    )


def join_square(block):
    block = block.astype(jnp.float32)
    return block[:, :1] + block[:, LANES // 2 : LANES // 2 + 1]


def push(source, target, send_sem, recv_sem, axis, peer):
    return pltpu.make_async_remote_copy(
        src_ref=source,
        dst_ref=target,
        send_sem=send_sem,
        recv_sem=recv_sem,
        device_id={axis: peer},
        device_id_type=MESH,
    )


def partner(axis, step):
    me, size = lax.axis_index(axis), lax.axis_size(axis)
    other, bit = me, 1
    while bit < size:
        if (step // bit) % 2:
            other = other + bit - 2 * bit * lax.rem(me // bit, 2)
        bit *= 2
    return other


def greet(axes):
    barrier = pltpu.get_barrier_semaphore()
    count = 0
    for axis in axes:
        for step in range(1, lax.axis_size(axis)):
            pl.semaphore_signal(
                barrier, inc=1, device_id={axis: partner(axis, step)}, device_id_type=MESH
            )
        count += lax.axis_size(axis) - 1
    pl.semaphore_wait(barrier, count)


def spread_own(buffer, send_sems, recv_sems, axis):
    me = lax.axis_index(axis)
    for step in range(lax.axis_size(axis) - 1, 0, -1):
        peer = partner(axis, step)
        push(
            buffer.at[me], buffer.at[me], send_sems.at[peer], recv_sems.at[me], axis, peer
        ).start()


def deal(source, buffer, send_sems, recv_sems, axis):
    me = lax.axis_index(axis)
    for step in range(lax.axis_size(axis) - 1, 0, -1):
        peer = partner(axis, step)
        push(
            source.at[peer], buffer.at[me], send_sems.at[peer], recv_sems.at[me], axis, peer
        ).start()


def take(buffer, send_sems, recv_sems, axis, step):
    peer = partner(axis, step)
    push(
        buffer.at[peer], buffer.at[peer], send_sems.at[peer], recv_sems.at[peer], axis, peer
    ).wait_recv()
    return peer


def take_all(buffer, send_sems, recv_sems, axis):
    for step in range(1, lax.axis_size(axis)):
        take(buffer, send_sems, recv_sems, axis, step)


def settle(buffer, send_sems, recv_sems, axis):
    me = lax.axis_index(axis)
    for step in range(1, lax.axis_size(axis)):
        peer = partner(axis, step)
        push(
            buffer.at[peer], buffer.at[peer], send_sems.at[peer], recv_sems.at[me], axis, peer
        ).wait_send()


def spread_gain(gain_ref):
    return jnp.broadcast_to(gain_ref[...], (PAD, gain_ref.shape[1]))


def block_codes(ids_ref, turned, block_rows):
    turned[...] = ids_ref[...].astype(jnp.float32).T
    first = pl.multiple_of(lax.axis_index("ty") * block_rows, block_rows)
    return turned[pl.ds(first, block_rows), :]


def gained_rows(blocks, rows, scaled_ref):
    square = jnp.zeros((rows, 1), jnp.float32)
    width = blocks.shape[2]
    for part in range(blocks.shape[0]):
        values = blocks[part, :rows, :].astype(jnp.float32)
        gain = blocks[part, rows : rows + PAD, :].astype(jnp.float32)[:1]
        square = square + jnp.sum(values * values, axis=1, keepdims=True)
        scaled_ref[:, part * width : (part + 1) * width] = (values * gain).astype(jnp.bfloat16)
    return square


def qkv_kernel(
    full_width, hidden_ref, gain_ref, ids_ref, weight_hbm, table_hbm, out_ref, words_ref,
    weight, table, turned, gathered, scaled, sums_out, sums_in, rows_out, rows_in, words_out,
    words_in, fetch_sem, g_send, g_recv, s_send, s_recv, r_send, r_recv, w_send, w_recv,
):
    me_tx, me_ty = lax.axis_index("tx"), lax.axis_index("ty")
    count_tx, count_ty = lax.axis_size("tx"), lax.axis_size("ty")
    rows = scaled.shape[0]
    columns = weight.shape[1]
    block_rows = rows // count_ty
    entries = table.shape[1]
    width = table.shape[2] // count_tx
    fetch = pltpu.make_async_copy(weight_hbm, weight, fetch_sem.at[0])
    fetch.start()
    fetch_table = pltpu.make_async_copy(table_hbm, table, fetch_sem.at[1])
    fetch_table.start()
    gathered[me_tx, :rows, :] = hidden_ref[...]
    gathered[me_tx, rows:, :] = spread_gain(gain_ref)
    greet(("tx", "ty"))
    spread_own(gathered, g_send, g_recv, "tx")
    codes = block_codes(ids_ref, turned, block_rows)
    entry = lax.broadcasted_iota(jnp.int32, (block_rows, entries), 1) + me_tx * entries
    fetch_table.wait()
    for k in range(STEPS - 1):
        found = (codes[:, k : k + 1].astype(jnp.int32) == entry).astype(jnp.float32)
        found = found.astype(jnp.bfloat16)
        for d in range(count_tx):
            words_out[d, k] = jnp.dot(
                found, table[k, :, d * width : (d + 1) * width], preferred_element_type=jnp.float32
            ).astype(jnp.bfloat16)
    take_all(gathered, g_send, g_recv, "tx")
    deal(words_out, words_in, w_send, w_recv, "tx")
    words_in[me_tx] = words_out[me_tx]
    square = gained_rows(gathered, rows, scaled)
    fetch.wait()
    tile = 512
    for start in range(0, columns, tile):
        part = jnp.dot(
            scaled[...], weight[:, start : start + tile], preferred_element_type=jnp.float32
        )
        sums_out[:, :, start : start + tile] = part.astype(jnp.bfloat16).reshape(
            count_ty, block_rows, tile
        )
    sums_out[:, :, columns:] = split_square(square).reshape(count_ty, block_rows, LANES)
    deal(sums_out, sums_in, s_send, s_recv, "ty")
    sums_in[me_ty] = sums_out[me_ty]
    take_all(sums_in, s_send, s_recv, "ty")
    square = jnp.zeros((block_rows, 1), jnp.float32)
    for part in range(count_ty):
        square = square + join_square(sums_in[part, :, columns:])
    scale = lax.rsqrt(square / full_width + epsilon)
    own_rows = block_rows // count_tx
    piece = columns // count_tx
    raw = []
    for q in range(count_tx):
        total = jnp.zeros((block_rows, piece), jnp.float32)
        for part in range(count_ty):
            total = total + sums_in[part, :, q * piece : (q + 1) * piece].astype(jnp.float32)
        raw.append(total * scale)
    for d in range(count_tx):
        rows_out[d] = jnp.concatenate(
            [part[d * own_rows : (d + 1) * own_rows] for part in raw], axis=0
        ).astype(jnp.bfloat16)
    deal(rows_out, rows_in, r_send, r_recv, "tx")
    rows_in[me_tx] = rows_out[me_tx]
    take_all(rows_in, r_send, r_recv, "tx")
    out_ref[...] = rows_in[...]
    take_all(words_in, w_send, w_recv, "tx")
    for k in range(STEPS - 1):
        word = words_in[0, k].astype(jnp.float32)
        for src in range(1, count_tx):
            word = word + words_in[src, k].astype(jnp.float32)
        words_ref[k] = word
    settle(gathered, g_send, g_recv, "tx")
    settle(words_in, w_send, w_recv, "tx")
    settle(sums_in, s_send, s_recv, "ty")
    settle(rows_in, r_send, r_recv, "tx")


def qkv_rows(hidden, gain, ids, qkv_weight, table, full_width, count_tx, count_ty):
    rows, part_width = hidden.shape
    columns = qkv_weight.shape[1]
    block_rows = rows // count_ty
    piece = columns // count_tx
    width = table.shape[2] // count_tx
    dma = pltpu.SemaphoreType.DMA
    bf16, f32 = jnp.bfloat16, jnp.float32
    inside = pl.BlockSpec(memory_space=pltpu.VMEM)
    outside = pl.BlockSpec(memory_space=pl.ANY)
    by_tx, by_ty = dma((count_tx,)), dma((count_ty,))
    return pl.pallas_call(
        functools.partial(qkv_kernel, full_width),
        out_shape=(
            jax.ShapeDtypeStruct((count_tx, block_rows, piece), bf16),
            jax.ShapeDtypeStruct((STEPS - 1, block_rows, width), f32),
        ),
        in_specs=[inside, inside, inside, outside, outside],
        out_specs=(inside, inside),
        scratch_shapes=[
            pltpu.VMEM(qkv_weight.shape, bf16),
            pltpu.VMEM(table.shape, bf16),
            pltpu.VMEM((rows, STEPS), f32),
            pltpu.VMEM((count_tx, rows + PAD, part_width), bf16),
            pltpu.VMEM((rows, count_tx * part_width), bf16),
            pltpu.VMEM((count_ty, block_rows, columns + LANES), bf16),
            pltpu.VMEM((count_ty, block_rows, columns + LANES), bf16),
            pltpu.VMEM((count_tx, block_rows, piece), bf16),
            pltpu.VMEM((count_tx, block_rows, piece), bf16),
            pltpu.VMEM((count_tx, STEPS - 1, block_rows, width), bf16),
            pltpu.VMEM((count_tx, STEPS - 1, block_rows, width), bf16),
            dma((2,)),
            by_tx, by_tx, by_ty, by_ty, by_tx, by_tx, by_tx, by_tx,
        ],
        compiler_params=pltpu.CompilerParams(
            collective_id=1, has_side_effects=True, vmem_limit_bytes=VMEM_BYTES
        ),
    )(hidden, gain, ids, qkv_weight, table)


def tail_kernel(
    full_width, att_ref, out_hbm, resid_ref, gain_ref, in_hbm, ids_ref, owners_ref,
    pre_ref, head_ref, words_ref, gate_hbm, up_hbm, down_hbm, table_hbm, hidden_ref, out_ref,
    out_w, in_w, gate, up, down, table, pieces, blocks, part_out, part_in, gathered, scaled,
    starts_out, starts_in, state, gate_sum, up_sum, pre, out, sums_out, sums_in, turned,
    ends, finals,
    w_sem, a_send, a_recv, b_send, b_recv, p_send, p_recv, g_send, g_recv, s_send, s_recv,
    pre_s, pre_r, out_s, out_r, sum_s, sum_r, end_s, end_r, fin_s, fin_r,
):
    me, me_ty = lax.axis_index("tx"), lax.axis_index("ty")
    count, count_ty = lax.axis_size("tx"), lax.axis_size("ty")
    rows, feature_width = resid_ref.shape
    block_rows, width = state.shape
    entries = table.shape[1]
    full = width * count
    fetch_out, fetch_in, *fetch_rest = [
        pltpu.make_async_copy(far, near, w_sem.at[i])
        for i, (far, near) in enumerate(
            (
                (out_hbm, out_w),
                (in_hbm, in_w),
                (gate_hbm, gate),
                (up_hbm, up),
                (down_hbm, down),
                (table_hbm, table),
            )
        )
    ]
    for fetch in [fetch_out, fetch_in] + fetch_rest:
        fetch.start()
    lane = lax.broadcasted_iota(jnp.int32, (block_rows, LANES), 1)
    entry = lax.broadcasted_iota(jnp.int32, (block_rows, entries), 1)
    codes = block_codes(ids_ref, turned, block_rows).astype(jnp.int32)
    code_lane = lax.broadcasted_iota(jnp.int32, codes.shape, 1)

    def chosen(k):
        code = jnp.sum(jnp.where(code_lane == k, codes, 0), axis=1, keepdims=True)
        return code - me * entries == entry

    pieces[me] = att_ref[me]
    greet(("tx", "ty"))
    deal(att_ref, pieces, a_send, a_recv, "tx")
    take_all(pieces, a_send, a_recv, "tx")
    piece = pieces.shape[2]
    own_rows = block_rows // count
    for q in range(count):
        blocks[me_ty, :, q * piece : (q + 1) * piece] = jnp.concatenate(
            [
                pieces[src].astype(jnp.float32)[q * own_rows : (q + 1) * own_rows]
                for src in range(count)
            ],
            axis=0,
        ).astype(jnp.bfloat16)
    spread_own(blocks, b_send, b_recv, "ty")
    take_all(blocks, b_send, b_recv, "ty")
    fetch_out.wait()
    attended = blocks[...].reshape(rows, blocks.shape[2])
    for d in range(count):
        part_out[d] = jnp.dot(
            attended,
            out_w[:, d * feature_width : (d + 1) * feature_width],
            preferred_element_type=jnp.float32,
        ).astype(jnp.bfloat16)
    deal(part_out, part_in, p_send, p_recv, "tx")
    part_in[me] = part_out[me]
    take_all(part_in, p_send, p_recv, "tx")
    total = resid_ref[...].astype(jnp.float32)
    for src in range(count):
        total = total + part_in[src].astype(jnp.float32)
    hidden = total.astype(jnp.bfloat16)
    hidden_ref[...] = hidden
    gathered[me, :rows, :] = hidden
    gathered[me, rows:, :] = spread_gain(gain_ref)
    spread_own(gathered, g_send, g_recv, "tx")
    take_all(gathered, g_send, g_recv, "tx")
    square = gained_rows(gathered, rows, scaled)
    fetch_in.wait()
    start = jnp.dot(scaled[...], in_w[...], preferred_element_type=jnp.float32)
    starts_out[:, :, :width] = start.astype(jnp.bfloat16).reshape(count_ty, block_rows, width)
    starts_out[:, :, width:] = split_square(square).reshape(count_ty, block_rows, LANES)
    deal(starts_out, starts_in, s_send, s_recv, "ty")
    starts_in[me_ty] = starts_out[me_ty]
    ends[me] = jnp.zeros(ends.shape[1:], jnp.float32)
    for fetch in fetch_rest:
        fetch.wait()
    take_all(starts_in, s_send, s_recv, "ty")
    total = jnp.zeros((block_rows, width), jnp.float32)
    square = jnp.zeros((block_rows, 1), jnp.float32)
    for src in range(count_ty):
        total = total + starts_in[src, :, :width].astype(jnp.float32)
        square = square + join_square(starts_in[src, :, width:])
    scale = lax.rsqrt(square / full_width + epsilon)
    state[...] = (total * scale).astype(jnp.bfloat16).astype(jnp.float32)

    def announce(buffer, k, values, send_sems, recv_sems):
        buffer[k, me] = values.astype(jnp.bfloat16)
        spread_own(buffer.at[k], send_sems.at[k], recv_sems.at[k], "tx")

    def gained(buffer, k, src, factor_ref):
        values = buffer[k, src].astype(jnp.float32)
        square = jnp.sum(values * values, axis=1, keepdims=True)
        columns = pl.ds(pl.multiple_of(src * width, width), width)
        factor = factor_ref[:, columns].astype(jnp.float32)
        return (values * factor).astype(jnp.bfloat16), square

    def score(k):
        logits = jnp.zeros((block_rows, entries), jnp.float32)
        square = jnp.zeros((block_rows, 1), jnp.float32)
        for step in range(count):
            if step:
                take(out.at[k], out_s.at[k], out_r.at[k], "tx", step)
            src = partner("tx", step)
            columns = pl.ds(pl.multiple_of(src * width, width), width)
            block, term = gained(out, k, src, head_ref)
            logits = logits + lax.dot_general(
                block,
                table[k, :, columns],
                (((1,), (1,)), ((), ())),
                preferred_element_type=jnp.float32,
            )
            square = square + term
        logits = logits * lax.rsqrt(square / full + epsilon)
        total = jnp.sum(jnp.exp(logits), axis=1, keepdims=True)
        picked = jnp.sum(jnp.where(chosen(k), logits, 0.0), axis=1, keepdims=True)
        ends[me, 0] = jnp.where(lane == k, total, ends[me, 0])
        ends[me, 1] = jnp.where(lane == k, picked, ends[me, 1])

    def one_step(k, carry):
        square = jnp.zeros((block_rows, 1), jnp.float32)
        for step in range(count):
            if step:
                take(pre.at[k], pre_s.at[k], pre_r.at[k], "tx", step)
            src = partner("tx", step)
            depth = pl.ds(pl.multiple_of(src * width, width), width)
            block, term = gained(pre, k, src, pre_ref)
            gate_part = jnp.dot(block, gate[depth, :], preferred_element_type=jnp.float32)
            up_part = jnp.dot(block, up[depth, :], preferred_element_type=jnp.float32)
            if step:
                gate_part = gate_sum[...] + gate_part
                up_part = up_sum[...] + up_part
            gate_sum[...] = gate_part
            up_sum[...] = up_part
            square = square + term
        scale = lax.rsqrt(square / full + epsilon)
        gate_part = gate_sum[...] * scale
        act = (gate_part / (1.0 + jnp.exp(-gate_part)) * (up_sum[...] * scale)).astype(jnp.bfloat16)
        for step in range(count - 1, -1, -1):
            peer = partner("tx", step)
            columns = pl.ds(pl.multiple_of(peer * width, width), width)
            part = jnp.dot(act, down[:, columns], preferred_element_type=jnp.float32)
            if step:
                sums_out[k, peer] = part.astype(jnp.bfloat16)
                push(
                    sums_out.at[k, peer], sums_in.at[k, me], sum_s.at[k, peer], sum_r.at[k, me],
                    "tx", peer,
                ).start()
            else:
                state[...] = state[...] + part

        @pl.when(k > 0)
        def _():
            score(k - 1)
            settle(pre.at[k - 1], pre_s.at[k - 1], pre_r.at[k - 1], "tx")
            settle(out.at[k - 1], out_s.at[k - 1], out_r.at[k - 1], "tx")
            settle(sums_in.at[k - 1], sum_s.at[k - 1], sum_r.at[k - 1], "tx")

        total = jnp.zeros((block_rows, width), jnp.float32)
        for step in range(1, count):
            src = take(sums_in.at[k], sum_s.at[k], sum_r.at[k], "tx", step)
            total = total + sums_in[k, src].astype(jnp.float32)
        settled = state[...] + total

        @pl.when(k < STEPS - 1)
        def _():
            entering = settled + embed_gain * words_ref[k]
            state[...] = entering
            announce(pre, k + 1, entering, pre_s, pre_r)

        announce(out, k, settled, out_s, out_r)
        return carry

    announce(pre, 0, state[...], pre_s, pre_r)
    lax.fori_loop(0, STEPS, one_step, 0)
    score(STEPS - 1)
    spread_own(ends, end_s, end_r, "tx")
    take_all(ends, end_s, end_r, "tx")
    total = ends[0, 0]
    picked = ends[0, 1]
    for src in range(1, count):
        total = total + ends[src, 0]
        picked = picked + ends[src, 1]
    finals[me_ty] = picked - jnp.log(jnp.where(lane < STEPS, total, 1.0))
    spread_own(finals, fin_s, fin_r, "ty")
    take_all(finals, fin_s, fin_r, "ty")
    owner = owners_ref[...]
    mine = owner == me_ty
    above = lax.broadcasted_iota(jnp.int32, (rows, rows), 0)
    below = lax.broadcasted_iota(jnp.int32, (rows, rows), 1)
    ahead = (above < below) & (above // block_rows == below // block_rows)
    rank = jnp.dot(
        mine.astype(jnp.float32).astype(jnp.bfloat16),
        ahead.astype(jnp.float32).astype(jnp.bfloat16),
        preferred_element_type=jnp.float32,
    ).astype(jnp.int32)
    slots = out_ref.shape[2]
    row = lax.broadcasted_iota(jnp.int32, (1, rows), 1)
    place = jnp.where(mine, row // block_rows * (slots // count_ty) + rank, -1)
    select = lax.broadcasted_iota(jnp.int32, (slots, rows), 0) == place
    placed = jnp.dot(
        select.astype(jnp.float32),
        finals[...].reshape(rows, LANES),
        precision=lax.Precision.HIGHEST,
        preferred_element_type=jnp.float32,
    )
    out_ref[0] = placed.T[:STEPS]
    settle(pieces, a_send, a_recv, "tx")
    settle(blocks, b_send, b_recv, "ty")
    settle(part_in, p_send, p_recv, "tx")
    settle(gathered, g_send, g_recv, "tx")
    settle(starts_in, s_send, s_recv, "ty")

    settle(out.at[STEPS - 1], out_s.at[STEPS - 1], out_r.at[STEPS - 1], "tx")
    settle(pre.at[STEPS - 1], pre_s.at[STEPS - 1], pre_r.at[STEPS - 1], "tx")
    settle(sums_in.at[STEPS - 1], sum_s.at[STEPS - 1], sum_r.at[STEPS - 1], "tx")
    settle(ends, end_s, end_r, "tx")
    settle(finals, fin_s, fin_r, "ty")


def tail_rows(
    attended, out_weight, residual, gain, in_weight, ids, owners, pre_gain, head_gain, words,
    mlp_gate, mlp_up, mlp_down, table, slots, full_width, count_tx, count_ty,
):
    rows, width = residual.shape
    block_rows = attended.shape[1]
    columns = in_weight.shape[1]
    hidden_units = mlp_gate.shape[1]
    dma = pltpu.SemaphoreType.DMA
    inside = pl.BlockSpec(memory_space=pltpu.VMEM)
    outside = pl.BlockSpec(memory_space=pl.ANY)
    bf16, f32 = jnp.bfloat16, jnp.float32
    each = (STEPS, count_tx)
    by_tx, by_ty = dma((count_tx,)), dma((count_ty,))
    return pl.pallas_call(
        functools.partial(tail_kernel, full_width),
        out_shape=(
            jax.ShapeDtypeStruct((rows, width), bf16),
            jax.ShapeDtypeStruct((1, STEPS, slots), f32),
        ),
        in_specs=[inside, outside, inside, inside, outside] + [inside] * 5 + [outside] * 4,
        out_specs=(inside, inside),
        scratch_shapes=[
            pltpu.VMEM(out_weight.shape, bf16),
            pltpu.VMEM(in_weight.shape, bf16),
            pltpu.VMEM(mlp_gate.shape, bf16),
            pltpu.VMEM(mlp_up.shape, bf16),
            pltpu.VMEM(mlp_down.shape, bf16),
            pltpu.VMEM(table.shape, bf16),
            pltpu.VMEM(attended.shape, bf16),
            pltpu.VMEM((count_ty, block_rows, out_weight.shape[0]), bf16),
            pltpu.VMEM((count_tx, rows, width), bf16),
            pltpu.VMEM((count_tx, rows, width), bf16),
            pltpu.VMEM((count_tx, rows + PAD, width), bf16),
            pltpu.VMEM((rows, count_tx * width), bf16),
            pltpu.VMEM((count_ty, block_rows, columns + LANES), bf16),
            pltpu.VMEM((count_ty, block_rows, columns + LANES), bf16),
            pltpu.VMEM((block_rows, columns), f32),
            pltpu.VMEM((block_rows, hidden_units), f32),
            pltpu.VMEM((block_rows, hidden_units), f32),
        ]
        + [pltpu.VMEM(each + (block_rows, columns), bf16)] * 4
        + [
            pltpu.VMEM((rows, STEPS), f32),
            pltpu.VMEM((count_tx, 2, block_rows, LANES), f32),
            pltpu.VMEM((count_ty, block_rows, LANES), f32),
            dma((6,)),
            by_tx, by_tx, by_ty, by_ty, by_tx, by_tx, by_tx, by_tx, by_ty, by_ty,
        ]
        + [dma(each)] * 6
        + [by_tx, by_tx, by_ty, by_ty],
        compiler_params=pltpu.CompilerParams(
            collective_id=2, has_side_effects=True, vmem_limit_bytes=VMEM_BYTES
        ),
    )(
        attended, out_weight, residual, gain, in_weight, ids, owners, pre_gain, head_gain, words,
        mlp_gate, mlp_up, mlp_down, table,
    )


def body(
    hidden_in,
    norm_gain,
    qkv_weight,
    qkv_bias,
    key_cache,
    value_cache,
    lengths,
    out_weight,
    final_gain,
    in_weight,
    owners,
    codebook_ids,
    mlp_gate,
    mlp_up,
    mlp_down,
    pre_gain,
    head_gain,
    codebook_table,
):
    count_tx = lax.axis_size("tx")
    count_ty = lax.axis_size("ty")
    own_rows = key_cache.shape[0]
    full_width = hidden_in.shape[1] * count_tx * count_ty
    ids = codebook_ids.T
    raw, words = qkv_rows(
        hidden_in, norm_gain[None], ids, qkv_weight, codebook_table, full_width, count_tx, count_ty
    )
    qkv_raw = (
        raw.reshape(count_tx, count_tx, own_rows, raw.shape[2])
        .transpose(2, 0, 1, 3)
        .reshape(own_rows, count_tx * count_tx * raw.shape[2])
    )
    qkv = qkv_raw.astype(jnp.float32) + qkv_bias.astype(jnp.float32)
    query_width = HEADS * HEAD_DIM
    key_width = KV_HEADS * HEAD_DIM
    query_heads = rotate(qkv[:, :query_width].reshape(own_rows, HEADS, HEAD_DIM), lengths)
    query_heads = (query_heads * HEAD_DIM ** (-0.5)).astype(jnp.bfloat16)
    new_key = rotate(
        qkv[:, query_width : query_width + key_width].reshape(own_rows, KV_HEADS, HEAD_DIM), lengths
    ).astype(jnp.bfloat16)
    new_value = (
        qkv[:, query_width + key_width :].reshape(own_rows, KV_HEADS, HEAD_DIM).astype(jnp.bfloat16)
    )
    attended = attend(query_heads, new_key, new_value, key_cache, value_cache, lengths)
    attended = (
        attended.reshape(own_rows, count_tx, count_tx, -1)
        .transpose(1, 2, 0, 3)
        .reshape(count_tx, count_tx * own_rows, -1)
    )
    capacity = max(2, 2 * own_rows * count_tx // count_ty)
    return tail_rows(
        attended,
        out_weight,
        hidden_in,
        final_gain[None],
        in_weight,
        ids,
        owners[None],
        pre_gain[None],
        head_gain[None],
        words,
        mlp_gate,
        mlp_up,
        mlp_down,
        codebook_table,
        count_ty * capacity,
        full_width,
        count_tx,
        count_ty,
    )


def solution(mesh):
    placed = (
        P(None, ("ty", "tx")),
        P(("ty", "tx")),
        P("ty", "tx"),
        P(),
        P(("ty", "tx"), None, None),
        P(("ty", "tx"), None, None),
        P(("ty", "tx")),
        P("tx", "ty"),
        P(("ty", "tx")),
        P("ty", "tx"),
        P(),
        P(),
        P(None, "tx"),
        P(None, "tx"),
        P("tx", None),
        P(),
        P(),
        P(None, "tx", None),
    )
    return jax.shard_map(
        body,
        mesh=mesh,
        in_specs=placed,
        out_specs=(P(None, ("ty", "tx")), P("ty", None, None)),
        check_vma=False,
    )
```
